128 devices in a mesh: dp: 32 (over y, x, core), seq: 4 (over z).
Axes of the slice: x: 4, y: 4, z: 4, core: 2. Of those that a mesh axis runs over, the one named last changes fastest.
Arguments:
- tokens: bfloat16 [16384, 1152], P(('dp', 'seq')), may hold values from -6 to 6
- cotangent: bfloat16 [16384, 1152], P(('dp', 'seq')), may hold values from -6 to 6
- segments: int32 [32, 2, 256], P('dp', None, 'seq'), may hold values from -1 to 63, as said below
- slot_source: int32 [32, 2, 256], P('dp', None, 'seq'), may hold values from 0 to 511, as said below
- first_gain: bfloat16 [1152], P(('dp', 'seq')), may hold values from 0.5 to 1.5
- query_weight: bfloat16 [1152, 1152], P(('dp', 'seq')), may hold values from -0.25 to 0.25
- key_projection: bfloat16 [1152, 384], P(('dp', 'seq')), may hold values from -0.25 to 0.25
- value_projection: bfloat16 [1152, 384], P(('dp', 'seq')), may hold values from -0.1875 to 0.1875
- output_weight: bfloat16 [1152, 1152], P(('dp', 'seq')), may hold values from -0.75 to 0.75
- second_gain: bfloat16 [1152], P(('dp', 'seq')), may hold values from 0.5 to 1.5
- gate_weight: bfloat16 [1152, 3072], P(('dp', 'seq')), may hold values from -0.1875 to 0.1875
- up_weight: bfloat16 [1152, 3072], P(('dp', 'seq')), may hold values from -0.1875 to 0.1875
- down_weight: bfloat16 [3072, 1152], P(('dp', 'seq')), may hold values from -0.109375 to 0.109375
Outputs:
- layer_output: bfloat16 [16384, 1152], P(('dp', 'seq'))
- gradient_tokens: float32 [16384, 1152], P(('dp', 'seq'))
- gradient_first: float32 [1152], P(('dp', 'seq'))
- gradient_query: float32 [1152, 1152], P(('dp', 'seq'))
- gradient_key: float32 [1152, 384], P(('dp', 'seq'))
- gradient_value: float32 [1152, 384], P(('dp', 'seq'))
- gradient_output: float32 [1152, 1152], P(('dp', 'seq'))
- gradient_second: float32 [1152], P(('dp', 'seq'))
- gradient_gate: float32 [1152, 3072], P(('dp', 'seq'))
- gradient_up: float32 [1152, 3072], P(('dp', 'seq'))
- gradient_down: float32 [3072, 1152], P(('dp', 'seq'))
The draws below stay inside these ranges and needn't reach their ends.
Inputs may be any that keep to these rules, and one draw needn't show every extreme that they name: `segments`: each buffer holds one sequence from slot 0, then one or more padding slots marked -1; sequence ids are distinct over all buffers. `slot_source`: over one index of dp a permutation of its 512 arrival rows; every sequence and every padding run occupies consecutive arrival rows in slot order.
All inputs are finite; a program needn't handle non-finite values.
Results may differ from the reference program's by a relative error of at most 0.017.
Values may be sent and summed in bfloat16 or wider, within the bound.
No kernel may reach another device: no remote copies, remote signals or barrier semaphores. Data moves between devices by JAX's collectives and lax.ppermute only.
A program may use at most 256 MiB of HBM per device.

```python
import jax
import jax.numpy as jnp
from jax import lax

MODEL_WIDTH = 1152
QUERY_HEADS = 18
KEY_VALUE_HEADS = 6
HEAD_SIZE = 64
FF = 3072
SLOTS = 256
MB = 2
TOKENS = 16384
N_DP = 32


def packing(key):
    folded = jax.random.fold_in(key, 31)
    key_pad, key_order = jax.random.split(folded, 2)
    buffers = N_DP * MB
    padding = jax.random.randint(key_pad, (buffers,), 1, SLOTS // 16 + 2).astype(jnp.int32)
    filled = SLOTS - padding
    lengths = jnp.stack([filled, padding], axis=1).astype(jnp.int32)
    group_keys = jax.random.split(key_order, N_DP)
    arrival_order = jax.vmap(lambda one_key: jax.random.permutation(one_key, 2 * MB))(group_keys).astype(jnp.int32)
    placing = jnp.argsort(arrival_order, axis=1, stable=True).astype(jnp.int32)
    unit_lengths = lengths.reshape(N_DP, 2 * MB)
    before = placing[:, None, :] < placing[:, :, None]
    offsets = jnp.sum(jnp.where(before, unit_lengths[:, None, :], 0), axis=2).astype(jnp.int32)
    bounds = jnp.cumsum(lengths, axis=1).astype(jnp.int32)
    run_start = bounds - lengths
    slot_index = jnp.arange(SLOTS).astype(jnp.int32)
    run_number = jnp.sum((slot_index[None, :, None] >= bounds[:, None, :1]).astype(jnp.int32), axis=2).astype(jnp.int32)
    inside = slot_index[None, :] - jnp.take_along_axis(run_start, run_number, axis=1)
    unit_index = (jnp.arange(buffers).astype(jnp.int32) % MB)[:, None] * 2 + run_number
    unit_offsets = jnp.take_along_axis(jnp.repeat(offsets, MB, axis=0), unit_index, axis=1)
    sources = (unit_offsets + inside).astype(jnp.int32).reshape(N_DP, MB, SLOTS)
    segment_ids = jnp.where(run_number == 1, -1, jnp.arange(buffers).astype(jnp.int32)[:, None] + 0 * run_number)
    return (segment_ids.astype(jnp.int32).reshape(N_DP, MB, SLOTS), sources)


def draw_segments(key, part):
    return packing(key)[0]


def draw_slot_source(key, part):
    return packing(key)[1]


def steps_of(stream_key, shape, shards, least, largest):
    def one(position, blocks):
        draws = jax.random.uniform(jax.random.fold_in(jax.random.fold_in(stream_key, 6), position), (blocks,), jnp.float32, least / len(shards), largest / len(shards))
        return jnp.repeat(jnp.exp(draws), shape[position] // blocks).reshape((-1,) + (1,) * (len(shape) - position - 1))

    level = one(*shards[0])
    for cut in shards[1:]:
        level = level * one(*cut)
    return level


def gaussian(rng, extent, scale, limit, cuts=(), kind=jnp.bfloat16):
    values = scale * jax.random.normal(rng, extent, jnp.float32)
    if cuts:
        values = values * steps_of(rng, extent, cuts, -0.22, 0.18)
    return jnp.clip(values, -limit, limit).astype(kind)


def setup_inputs(seed: int = 0) -> dict:
    arg_keys = jax.random.split(jax.random.key(seed), 14)
    return {
        "tokens": gaussian(arg_keys[0], (TOKENS, MODEL_WIDTH), 1.0, 6.0, ((0, 128),)),
        "cotangent": gaussian(arg_keys[1], (TOKENS, MODEL_WIDTH), 1.0, 6.0, ((0, 128),)),
        "segments": draw_segments(jax.random.fold_in(arg_keys[13], 71), 0),
        "slot_source": draw_slot_source(jax.random.fold_in(arg_keys[13], 71), 0),
        "first_gain": jnp.clip(1.0 + 0.1 * jax.random.normal(arg_keys[4], (MODEL_WIDTH,), jnp.float32), 0.5, 1.5).astype(jnp.bfloat16),
        "query_weight": gaussian(arg_keys[5], (MODEL_WIDTH, QUERY_HEADS * HEAD_SIZE), (MODEL_WIDTH // 2) ** -0.5, 0.25, ((0, 128),)),
        "key_projection": gaussian(arg_keys[6], (MODEL_WIDTH, KEY_VALUE_HEADS * HEAD_SIZE), (MODEL_WIDTH // 2) ** -0.5, 0.25, ((0, 128),)),
        "value_projection": gaussian(arg_keys[7], (MODEL_WIDTH, KEY_VALUE_HEADS * HEAD_SIZE), MODEL_WIDTH ** -0.5, 0.1875, ((0, 128),)),
        "output_weight": gaussian(arg_keys[8], (QUERY_HEADS * HEAD_SIZE, MODEL_WIDTH), (QUERY_HEADS * HEAD_SIZE // 16) ** -0.5, 0.75, ((0, 128),)),
        "second_gain": jnp.clip(1.0 + 0.1 * jax.random.normal(arg_keys[9], (MODEL_WIDTH,), jnp.float32), 0.5, 1.5).astype(jnp.bfloat16),
        "gate_weight": gaussian(arg_keys[10], (MODEL_WIDTH, FF), MODEL_WIDTH ** -0.5, 0.1875, ((0, 128),)),
        "up_weight": gaussian(arg_keys[11], (MODEL_WIDTH, FF), MODEL_WIDTH ** -0.5, 0.1875, ((0, 128),)),
        "down_weight": gaussian(arg_keys[12], (FF, MODEL_WIDTH), FF ** -0.5, 0.109375, ((0, 128),)),
    }


EPS = 1e-05
THETA = 10000.0
HIGH = lax.Precision.HIGHEST

@jax.custom_vjp
def lower_precision(v):
    return lax.optimization_barrier(v.astype(jnp.bfloat16)).astype(jnp.float32)

@jax.custom_vjp
def lower_precision_backward(v):
    return v

def low_keep(v):
    return (lower_precision(v), None)

def low_pass(kept, grad):
    return (grad,)

def back_keep(v):
    return (v, None)

def back_low(kept, grad):
    return (lower_precision(grad),)
lower_precision.defvjp(low_keep, low_pass)
lower_precision_backward.defvjp(back_keep, back_low)

def matrix_multiply(left, right):
    return jnp.dot(left, right, precision=HIGH, preferred_element_type=jnp.float32)

def rope_tables(positions):
    half_dim = HEAD_SIZE // 2
    frequency = THETA ** (-(jnp.arange(half_dim).astype(jnp.float32) * 2.0 / HEAD_SIZE))
    angles = positions.astype(jnp.float32)[:, None] * frequency[None, :]
    return (jnp.cos(angles), jnp.sin(angles))

def rotary_apply(value_states, cosine_table, sine_table):
    half_dim = HEAD_SIZE // 2
    first_half = value_states[..., :half_dim]
    second_half = value_states[..., half_dim:]
    cos_heads = cosine_table[:, None, :]
    sin_heads = sine_table[:, None, :]
    return jnp.concatenate([first_half * cos_heads - second_half * sin_heads, first_half * sin_heads + second_half * cos_heads], axis=-1)

def layer(params, inputs, cosine_table, sine_table, allowed):
    gain_one, query_w, key_matrix, value_matrix, output_w, gain_two, gate_w, up_w, down_w = params
    token_length = inputs.shape[0]
    scale_one = lax.rsqrt(lax.optimization_barrier(jnp.mean(inputs * inputs, axis=-1, keepdims=True)) + EPS)
    hidden_first = lower_precision(inputs * scale_one * gain_one)
    query_states = lower_precision_backward(matrix_multiply(hidden_first, query_w)).reshape(token_length, QUERY_HEADS, HEAD_SIZE)
    key_states = lower_precision_backward(matrix_multiply(hidden_first, key_matrix)).reshape(token_length, KEY_VALUE_HEADS, HEAD_SIZE)
    value_states = lower_precision(lower_precision_backward(matrix_multiply(hidden_first, value_matrix))).reshape(token_length, KEY_VALUE_HEADS, HEAD_SIZE)
    query_states = lower_precision(rotary_apply(query_states, cosine_table, sine_table)).reshape(token_length, KEY_VALUE_HEADS, QUERY_HEADS // KEY_VALUE_HEADS, HEAD_SIZE)
    key_states = lower_precision(rotary_apply(key_states, cosine_table, sine_table))
    scores = lower_precision_backward(jnp.einsum('qhgd,khd->hgqk', query_states, key_states, precision=HIGH) * HEAD_SIZE ** (-0.5))
    scores = jnp.where(allowed, scores, -1e+30)
    weights = jax.nn.softmax(scores, axis=-1)
    mixed = jnp.einsum('hgqk,khd->qhgd', lower_precision(weights), value_states, precision=HIGH).reshape(token_length, QUERY_HEADS * HEAD_SIZE)
    mixed = lower_precision(lower_precision_backward(mixed))
    residual = inputs + lower_precision_backward(matrix_multiply(mixed, output_w))
    scale_two = lax.rsqrt(lax.optimization_barrier(jnp.mean(residual * residual, axis=-1, keepdims=True)) + EPS)
    hidden_two = lower_precision(residual * scale_two * gain_two)
    gate = lower_precision_backward(matrix_multiply(hidden_two, gate_w))
    up_values = lower_precision_backward(matrix_multiply(hidden_two, up_w))
    inner = lower_precision(jax.nn.silu(gate) * up_values)
    return residual + lower_precision_backward(matrix_multiply(inner, down_w))

def reference(tokens, cotangent, segments, slot_source, first_gain, query_weight, key_projection, value_projection, output_weight, second_gain, gate_weight, up_weight, down_weight):
    params = tuple((weight.astype(jnp.float32) for weight in (first_gain, query_weight, key_projection, value_projection, output_weight, second_gain, gate_weight, up_weight, down_weight)))
    group_rows = MB * SLOTS
    offsets = (jnp.arange(N_DP).astype(jnp.int32) * group_rows)[:, None, None]
    sources = (slot_source + offsets).reshape(N_DP * MB, SLOTS).astype(jnp.int32)
    buffer_ids = segments.reshape(N_DP * MB, SLOTS)
    inputs_all = tokens.astype(jnp.float32)
    upstream = cotangent.astype(jnp.float32)
    slot_index = jnp.arange(SLOTS).astype(jnp.int32)

    def one_buffer(running, packed):
        where_from, buffer_seg = packed
        same = buffer_seg[:, None] == buffer_seg[None, :]
        starts = jnp.argmax(same, axis=1).astype(jnp.int32)
        cosine_table, sine_table = rope_tables(slot_index - starts)
        allowed = same & (slot_index[None, :] <= slot_index[:, None])
        inputs = jnp.take(inputs_all, where_from, axis=0)
        outputs, pullback = jax.vjp(lambda weights, value_states: layer(weights, value_states, cosine_table, sine_table, allowed), params, inputs)
        weight_grads, input_grads = pullback(jnp.take(upstream, where_from, axis=0))
        running = tuple((current + addend for current, addend in zip(running, weight_grads)))
        return (running, (outputs.astype(jnp.bfloat16), input_grads))
    initial = tuple((jnp.zeros(weight.shape, jnp.float32) for weight in params))
    totals, (outputs, input_grads) = lax.scan(one_buffer, initial, (sources, buffer_ids))
    flat_sources = sources.reshape(-1)
    layer_output = jnp.zeros((N_DP * group_rows, MODEL_WIDTH), jnp.bfloat16).at[flat_sources].set(outputs.reshape(-1, MODEL_WIDTH))
    gradient_tokens = jnp.zeros((N_DP * group_rows, MODEL_WIDTH), jnp.float32).at[flat_sources].set(input_grads.reshape(-1, MODEL_WIDTH))
    return (layer_output, gradient_tokens, totals[0], totals[1], totals[2], totals[3], totals[4], totals[5], totals[6], totals[7], totals[8])
```

```python
import jax
import jax.numpy as jnp
from jax import lax
from jax.experimental import pallas as pl
from jax.experimental.pallas import tpu as pltpu
from jax.sharding import Mesh
from jax.sharding import PartitionSpec as P

HEAD = 64
EPS = 1e-05
THETA = 10000.0
BF = jnp.bfloat16
F32 = jnp.float32
ALL = ("y", "x", "c", "z")
COLUMN = ("c", "z")
PLANE = ("y", "x")
RANKS, PLANES, DEPTHS = 8, 16, 4
PARAMS = pltpu.CompilerParams(vmem_limit_bytes=56 * 1024 * 1024)


def dot(left, right):
    return jnp.dot(left, right, preferred_element_type=F32)


def dot_nt(left, right):
    return lax.dot_general(left, right, (((1,), (1,)), ((), ())), preferred_element_type=F32)


def dot_tn(left, right):
    return lax.dot_general(left, right, (((0,), (0,)), ((), ())), preferred_element_type=F32)


def dot_tt(left, right):
    return lax.dot_general(left, right, (((0,), (1,)), ((), ())), preferred_element_type=F32)


def exchange(value):
    return lax.ppermute(value, "c", [(0, 1), (1, 0)])


def deal(value, axes):
    return lax.all_to_all(value, axes, 0, 0, tiled=True)


def spread(value, axes, count):
    return deal(jnp.broadcast_to(value[None], (count,) + value.shape), axes)


def after(value, earlier):
    return lax.optimization_barrier((value, earlier))[0]


def from_depth(value, step):
    return lax.ppermute(value, "z", [(i, (i - step) % DEPTHS) for i in range(DEPTHS)])


def gather_depths(value):
    return [value, from_depth(value, 1), from_depth(value, 3), from_depth(value, 2)]


def scatter_depths(blocks):
    return [blocks[0], from_depth(blocks[2], 1), from_depth(blocks[1], 3), from_depth(blocks[3], 2)]


def in_depth_order(blocks, depth):
    doubled = jnp.stack([blocks[0], blocks[1], blocks[3], blocks[2]] * 2)
    return lax.dynamic_slice_in_dim(doubled, (DEPTHS - depth) % DEPTHS, DEPTHS, axis=0)


def by_step(stacked, depth):
    return [
        lax.dynamic_index_in_dim(stacked, (depth + step) % DEPTHS, axis=0, keepdims=False)
        for step in (0, 1, 3, 2)
    ]


def rope(value, cosine, sine):
    pairs = value.reshape(-1, 2, HEAD // 2, value.shape[1])
    first, second = pairs[:, 0], pairs[:, 1]
    return jnp.stack(
        [first * cosine - second * sine, first * sine + second * cosine], axis=1
    ).reshape(value.shape)


def norm_back(grad, normed, scale):
    return scale * (grad - normed * jnp.mean(grad * normed, axis=-1, keepdims=True))


def weight_gradient(left, right, block):
    rows, out_rows = left.shape
    columns = right.shape[1]

    def kernel(left_ref, right_ref, out_ref):
        out_ref[...] = dot_tn(left_ref[...], right_ref[...]).astype(BF)

    return pl.pallas_call(
        kernel,
        grid=(out_rows // block,),
        in_specs=[
            pl.BlockSpec((rows, block), lambda i: (0, i)),
            pl.BlockSpec((rows, columns), lambda i: (0, 0)),
        ],
        out_specs=pl.BlockSpec((block, columns), lambda i: (i, 0)),
        out_shape=jax.ShapeDtypeStruct((out_rows, columns), BF),
        compiler_params=PARAMS,
        cost_estimate=pl.CostEstimate(
            flops=2 * rows * out_rows * columns,
            bytes_accessed=2 * (rows * out_rows + rows * columns + out_rows * columns),
            transcendentals=0,
        ),
    )(left, right)


def on_device(
    tokens,
    cotangent,
    segments,
    slot_source,
    first_gain,
    query_weight,
    key_projection,
    value_projection,
    output_weight,
    second_gain,
    gate_weight,
    up_weight,
    down_weight,
):
    core, depth = lax.axis_index("c"), lax.axis_index("z")
    rows, width = tokens.shape
    own = query_weight.shape[0]
    q_cut, k_cut = query_weight.shape[1] // RANKS, key_projection.shape[1] // RANKS
    hidden = gate_weight.shape[1]
    rank_rows = down_weight.shape[0]
    rank_width = hidden // RANKS
    third = width // 3
    half = width // 2
    cut = q_cut + 2 * k_cut
    scale = HEAD ** (-0.5)

    def by_core(first, second):
        return jnp.where(core == 0, first, second)

    def by_rank(weight):
        return (
            weight.reshape(own, PLANES, RANKS, rank_rows)
            .transpose(2, 0, 1, 3)
            .reshape(RANKS, own, rank_width)
        )

    def from_ranks(blocks):
        return (
            blocks.reshape(RANKS, own, PLANES, rank_rows)
            .transpose(1, 2, 0, 3)
            .reshape(own, hidden)
        )

    def columns_by_rank(weight):
        return weight.reshape(own, RANKS, -1).transpose(1, 0, 2)

    def repeated(weight):
        return jnp.broadcast_to(weight[None], (RANKS,) + weight.shape)

    is_pad = segments[0] == -1
    filled = jnp.sum((~is_pad).astype(jnp.int32), axis=1)
    source = slot_source[0]
    slots = jnp.arange(source.shape[1])[None]
    pad_source = jnp.sum(jnp.where(slots == filled[:, None], source, 0), axis=1)
    marks = jnp.concatenate(
        [filled, source[:, 0] // 2, source[:, 0] % 2, pad_source // 2, pad_source % 2]
    ).astype(BF)
    gains = jnp.concatenate(
        [
            first_gain[:, None],
            second_gain[:, None],
            jnp.broadcast_to(marks[None], (own, marks.shape[0])),
            jnp.zeros((own, 256 - cut - 2 - marks.shape[0]), BF),
        ],
        axis=1,
    )
    parcels = jnp.concatenate(
        [
            columns_by_rank(query_weight),
            columns_by_rank(key_projection),
            columns_by_rank(value_projection),
            repeated(gains),
            by_rank(gate_weight),
            by_rank(up_weight),
            repeated(output_weight),
        ],
        axis=2,
    )
    column = deal(parcels, COLUMN).reshape(RANKS * own, -1)
    down_blocks = down_weight.reshape(rank_rows, 3, third).transpose(1, 0, 2).reshape(3 * rank_rows, third)
    later = jnp.concatenate([column[:, 256:1024], down_blocks, column[:, 1024:]], axis=1)
    attention_w = spread(column[:, :256], PLANE, PLANES).reshape(width, 256)
    later_w = lax.all_gather(later, PLANE, axis=0, tiled=True)
    ffn_w = later_w[:, : 2 * rank_width]
    down_w = (
        later_w[:, 2 * rank_width : 2 * rank_width + third]
        .reshape(PLANES, 3, rank_rows, third)
        .transpose(0, 2, 1, 3)
        .reshape(rank_width, width)
    )
    output_w = later_w[:, 2 * rank_width + third :]
    gain_one = attention_w[:, cut].astype(F32)
    gain_two = attention_w[:, cut + 1].astype(F32)
    attention_w = attention_w[:, :cut]

    marks = column.reshape(2, DEPTHS, own, -1)[:, :, 0, cut + 2 : cut + 12].astype(jnp.int32)
    marks = by_core(marks[0], marks[1]).reshape(DEPTHS, 5, 2)
    padded = marks[:, 0] < slots.shape[1]
    earlier_padded = jnp.concatenate([jnp.zeros((1, 2), bool), padded[:-1]])
    first_padded = padded & ~earlier_padded
    pad_starts = jnp.sum(
        jnp.where(first_padded, marks[:, 3] * 2 + marks[:, 4], 0), axis=0
    )
    starts = jnp.concatenate([marks[0, 1] * 2 + marks[0, 2], pad_starts])
    group_rows = jnp.arange(DEPTHS * rows)
    run_start = jnp.max(
        jnp.where(starts[None, :] <= group_rows[:, None], starts[None, :], 0), axis=1
    )
    own_start = lax.dynamic_slice_in_dim(run_start, depth * rows, rows, axis=0)
    own_rows = depth * rows + jnp.arange(rows)
    frequency = THETA ** (-(jnp.arange(HEAD // 2).astype(F32) * 2.0 / HEAD))
    angles = frequency[:, None] * (group_rows - run_start).astype(F32)[None, :]
    cosine, sine = jnp.cos(angles), jnp.sin(angles)
    own_cosine = lax.dynamic_slice_in_dim(cosine, depth * rows, rows, axis=1)
    own_sine = lax.dynamic_slice_in_dim(sine, depth * rows, rows, axis=1)
    allowed = (own_start[:, None] == run_start[None, :]) & (group_rows[None, :] <= own_rows[:, None])

    def column_rows(value):
        mine = jnp.stack(gather_depths(value))
        return jnp.concatenate([mine, exchange(mine)], axis=0).reshape(-1, width)

    def column_sum(partial):
        partial = partial.reshape(2, DEPTHS, rows, width)
        mine = partial[0] + exchange(partial[1].astype(BF)).astype(F32)
        received = scatter_depths([mine[0]] + [mine[i].astype(BF) for i in range(1, DEPTHS)])
        return sum(block.astype(F32) for block in received)

    def column_deal(mine, theirs):
        both = jnp.stack([mine, exchange(theirs)], axis=1)
        received = scatter_depths(by_step(both, depth))
        return in_depth_order(received, depth).transpose(1, 0, 2, 3)

    inputs_all = column_rows(after(tokens, column)).astype(F32)
    scale_all = lax.rsqrt(jnp.mean(inputs_all * inputs_all, axis=-1, keepdims=True) + EPS)
    hidden_one = (inputs_all * scale_all * gain_one).astype(BF)
    projected = dot_tt(attention_w, hidden_one).astype(BF)
    projected = projected.reshape(cut, 2, DEPTHS, rows).transpose(2, 0, 1, 3)
    projected = in_depth_order(projected, depth).transpose(1, 2, 0, 3)
    kv_part = projected[q_cut:].transpose(1, 2, 0, 3).reshape(2, 1, DEPTHS * 2 * k_cut, rows)
    parcels = jnp.concatenate(
        [
            projected[:q_cut].transpose(1, 2, 0, 3),
            jnp.broadcast_to(kv_part, (2, DEPTHS) + kv_part.shape[2:]),
        ],
        axis=2,
    )
    parcels = column_deal(parcels[0], parcels[1])
    upstream_rows = column_rows(after(cotangent, parcels))
    query = parcels[:, :, :q_cut].reshape(-1, rows).astype(F32)
    kv_part = parcels[:, :, q_cut:].reshape(2, DEPTHS, DEPTHS, 2, k_cut, rows)
    kv_part = kv_part.transpose(3, 0, 1, 4, 2, 5).reshape(2, RANKS * k_cut, DEPTHS * rows)
    heads_kv = RANKS * k_cut // HEAD
    group = q_cut // k_cut
    query = rope(query, own_cosine, own_sine).astype(BF).reshape(heads_kv, group, HEAD, rows)
    key = rope(kv_part[0].astype(F32), cosine, sine).astype(BF).reshape(heads_kv, HEAD, -1)
    value = kv_part[1].reshape(heads_kv, HEAD, -1)
    scores = jnp.einsum("hgdq,hdk->hgqk", query, key, preferred_element_type=F32) * scale
    scores = jnp.where(allowed, scores, -1e30)
    peak = jnp.max(scores, axis=-1, keepdims=True)
    weights = jnp.exp(scores - peak)
    weights = weights / jnp.sum(weights, axis=-1, keepdims=True)
    weights_low = weights.astype(BF)
    mixed = jnp.einsum("hgqk,hdk->hgdq", weights_low, value, preferred_element_type=F32)
    mixed = mixed.astype(BF).reshape(-1, rows)

    def natural(value):
        return by_core(value, jnp.concatenate([value[half:], value[:half]], axis=0))

    mixed = natural(mixed)

    residual = tokens.astype(F32) + dot_tn(mixed, output_w)
    scale_two = lax.rsqrt(jnp.mean(residual * residual, axis=-1, keepdims=True) + EPS)
    normed_two = residual * scale_two
    hidden_rows = column_rows((normed_two * gain_two).astype(BF))
    expanded = dot(hidden_rows, ffn_w)
    gate, up_values = expanded[:, :rank_width], expanded[:, rank_width:]
    gate_sigmoid = jax.nn.sigmoid(gate)
    activated = gate * gate_sigmoid
    inner = (activated * up_values).astype(BF)
    grad_inner = dot_nt(upstream_rows, down_w)
    grad_up_rows = (grad_inner * activated).astype(BF)
    grad_gate_rows = (
        grad_inner * up_values * gate_sigmoid * (1.0 + gate * (1.0 - gate_sigmoid))
    ).astype(BF)
    grad_expanded = jnp.concatenate([grad_gate_rows, grad_up_rows], axis=1)
    grad_hidden_two = column_sum(dot_nt(grad_expanded, ffn_w))
    grad_ffn = weight_gradient(hidden_rows, grad_expanded, 384)
    grad_down = weight_gradient(inner, upstream_rows, 384)
    grad_down = (
        grad_down.reshape(PLANES, rank_rows, 3, third).transpose(0, 2, 1, 3).reshape(width, third)
    )
    def plane_sum(value):
        value = deal(value.reshape(PLANES, RANKS * own, -1), PLANE)
        return jnp.sum(value.astype(F32), axis=0)

    ffn_sum = plane_sum(jnp.concatenate([grad_ffn, grad_down], axis=1))

    grad_residual = cotangent.astype(F32) + norm_back(
        grad_hidden_two * gain_two, normed_two, scale_two
    )
    residual_low = grad_residual.astype(BF)
    layer_output = dot(after(inner, residual_low), down_w)
    layer_output = (residual + column_sum(layer_output)).astype(BF)
    grad_output = dot(mixed, residual_low)
    grad_output_own = by_core(grad_output[:, :half], grad_output[:, half:])
    grad_output_other = by_core(grad_output[:, half:], grad_output[:, :half]).astype(BF)
    grad_output = (grad_output_own + exchange(grad_output_other).astype(F32)).astype(BF)

    grad_mixed = natural(dot_nt(output_w, residual_low).astype(BF))
    grad_mixed = grad_mixed.reshape(heads_kv, group, HEAD, rows)
    grad_weights = jnp.einsum("hgdq,hdk->hgqk", grad_mixed, value, preferred_element_type=F32)
    centre = jnp.sum(weights * grad_weights, axis=-1, keepdims=True)
    grad_scores = (weights * (grad_weights - centre)).astype(BF)
    grad_query = jnp.einsum("hgqk,hdk->hgdq", grad_scores, key, preferred_element_type=F32)
    grad_key = jnp.einsum("hgqk,hgdq->hdk", grad_scores, query, preferred_element_type=F32)
    grad_value = jnp.einsum("hgqk,hgdq->hdk", weights_low, grad_mixed, preferred_element_type=F32)
    grad_query = rope(grad_query.reshape(-1, rows) * scale, own_cosine, -own_sine).astype(BF)
    grad_key = rope(grad_key.reshape(RANKS * k_cut, -1) * scale, cosine, -sine).astype(BF)
    grad_value = grad_value.reshape(RANKS * k_cut, -1).astype(BF)
    kv_part = jnp.stack([grad_key, grad_value]).reshape(2, 2, DEPTHS, k_cut, DEPTHS, rows)
    kv_part = kv_part.transpose(1, 2, 4, 0, 3, 5).reshape(2, DEPTHS, -1, rows)
    parcels = jnp.concatenate(
        [grad_query.reshape(2, DEPTHS, q_cut, rows), kv_part], axis=2
    )
    parcels = column_deal(parcels[0], parcels[1])
    grad_query = parcels[:, :, :q_cut].transpose(2, 0, 1, 3).reshape(q_cut, -1)
    grad_kv = jnp.sum(parcels[:, :, q_cut:].astype(F32), axis=1).astype(BF)
    grad_kv = grad_kv.reshape(2, DEPTHS, 2 * k_cut, rows).transpose(2, 0, 1, 3).reshape(2 * k_cut, -1)
    grad_projected = jnp.concatenate([grad_query, grad_kv], axis=0)
    grad_projected = jnp.stack(
        by_step(grad_projected.reshape(-1, 2, DEPTHS, rows).transpose(2, 0, 1, 3), depth), axis=2
    ).reshape(cut, -1)
    grad_attention = lax.dot_general(
        hidden_one, grad_projected, (((0,), (1,)), ((), ())), preferred_element_type=F32
    ).astype(BF)
    grad_hidden_one = column_sum(dot_tt(grad_projected, attention_w))
    own_inputs = tokens.astype(F32)
    own_scale = lax.rsqrt(jnp.mean(own_inputs * own_inputs, axis=-1, keepdims=True) + EPS)
    gradient_tokens = grad_residual + norm_back(
        grad_hidden_one * gain_one, own_inputs * own_scale, own_scale
    )

    attention_sum = plane_sum(jnp.concatenate([grad_attention, grad_output], axis=1))
    summed = jnp.concatenate([ffn_sum[:, : 2 * rank_width], attention_sum], axis=1).astype(BF)
    summed = deal(summed.reshape(RANKS, own, -1), COLUMN).astype(F32)
    early, attention_sum = summed[:, :, : 2 * rank_width], summed[:, :, 2 * rank_width :]
    output_sum = jnp.sum(attention_sum[:, :, cut:].reshape(2, DEPTHS, own, half), axis=1)
    grad_o = output_sum.transpose(1, 0, 2).reshape(own, -1)

    def together(blocks):
        return blocks.transpose(1, 0, 2).reshape(own, -1)

    grad_q = together(attention_sum[:, :, :q_cut])
    grad_k = together(attention_sum[:, :, q_cut : q_cut + k_cut])
    grad_v = together(attention_sum[:, :, q_cut + k_cut : cut])
    grad_g = from_ranks(early[:, :, :rank_width])
    grad_u = from_ranks(early[:, :, rank_width : 2 * rank_width])
    grad_d = (
        ffn_sum[:, 2 * rank_width :]
        .reshape(3, rank_rows, third)
        .transpose(1, 0, 2)
        .reshape(rank_rows, width)
    )
    gain_grad_one = (
        jnp.sum(grad_q * query_weight.astype(F32), axis=1)
        + jnp.sum(grad_k * key_projection.astype(F32), axis=1)
        + jnp.sum(grad_v * value_projection.astype(F32), axis=1)
    ) / first_gain.astype(F32)
    gain_grad_two = (
        jnp.sum(grad_g * gate_weight.astype(F32), axis=1)
        + jnp.sum(grad_u * up_weight.astype(F32), axis=1)
    ) / second_gain.astype(F32)
    return (
        layer_output,
        gradient_tokens,
        gain_grad_one,
        grad_q,
        grad_k,
        grad_v,
        grad_o,
        gain_grad_two,
        grad_g,
        grad_u,
        grad_d,
    )


def solution(mesh):
    grid = Mesh(mesh.devices.reshape(4, 4, 2, 4), ALL)
    rows = P(ALL, None)
    flat = P(ALL)
    slots = P(("y", "x", "c"), None, "z")
    return jax.shard_map(
        on_device,
        mesh=grid,
        in_specs=(rows, rows, slots, slots, flat, rows, rows, rows, rows, flat, rows, rows, rows),
        out_specs=(rows, rows, flat, rows, rows, rows, rows, flat, rows, rows, rows),
        check_vma=False,
    )
```

```python
import jax
import jax.numpy as jnp
from jax import lax
from jax.experimental import pallas as pl
from jax.experimental.pallas import tpu as pltpu
from jax.sharding import Mesh
from jax.sharding import PartitionSpec as P

HEAD = 64
EPS = 1e-05
THETA = 10000.0
BF = jnp.bfloat16
F32 = jnp.float32
ALL = ("y", "x", "c", "z")
COLUMN = ("c", "z")
PLANE = ("y", "x")
RANKS, PLANES, DEPTHS = 8, 16, 4
PARAMS = pltpu.CompilerParams(vmem_limit_bytes=56 * 1024 * 1024)


def dot(left, right):
    return jnp.dot(left, right, preferred_element_type=F32)


def dot_nt(left, right):
    return lax.dot_general(left, right, (((1,), (1,)), ((), ())), preferred_element_type=F32)


def dot_tn(left, right):
    return lax.dot_general(left, right, (((0,), (0,)), ((), ())), preferred_element_type=F32)


def exchange(value):
    return lax.ppermute(value, "c", [(0, 1), (1, 0)])


def deal(value, axes):
    return lax.all_to_all(value, axes, 0, 0, tiled=True)


def after(value, earlier):
    return lax.optimization_barrier((value, earlier))[0]


def from_depth(value, step):
    return lax.ppermute(value, "z", [(i, (i - step) % DEPTHS) for i in range(DEPTHS)])


def gather_depths(value):
    return [value, from_depth(value, 1), from_depth(value, 3), from_depth(value, 2)]


def scatter_depths(blocks):
    return [blocks[0], from_depth(blocks[2], 1), from_depth(blocks[1], 3), from_depth(blocks[3], 2)]


STEPS = (0, 1, 3, 2)


def entire(shape):
    return pl.BlockSpec(shape, lambda i: (0,) * len(shape))


def run(
    kernel, outs, values, scalars=None, scratch=(), vmem=16, flops=0, read=None, fetch=False
):
    whole = pl.BlockSpec(memory_space=pltpu.VMEM)
    specs = [entire(value.shape) if fetch else whole for value in values] if read is None else list(read)
    if scalars is not None:
        values = [scalars] + list(values)
        specs = [pl.BlockSpec(memory_space=pltpu.SMEM)] + specs
    shapes = [jax.ShapeDtypeStruct(shape, dtype) for shape, dtype in outs]
    size = sum(v.size * v.dtype.itemsize for v in values)
    size += sum(o.size * o.dtype.itemsize for o in shapes)
    return pl.pallas_call(
        kernel,
        grid=(1,),
        in_specs=specs,
        out_specs=[entire(shape) if fetch else whole for shape, _ in outs],
        out_shape=shapes,
        scratch_shapes=list(scratch),
        compiler_params=pltpu.CompilerParams(vmem_limit_bytes=vmem * 1024 * 1024),
        cost_estimate=pl.CostEstimate(
            flops=flops, bytes_accessed=size, transcendentals=0
        ),
    )(*values)


WHOLE = pl.BlockSpec(memory_space=pltpu.VMEM)
AWAY = pl.BlockSpec(memory_space=pl.ANY)


def halves(count, which, shape):
    return [pl.BlockSpec((1,) + shape, lambda i: (which, 0, 0))] * count


def turned(value, cosine, sine):
    first, second = value[: HEAD // 2], value[HEAD // 2 :]
    return jnp.concatenate(
        [first * cosine - second * sine, first * sine + second * cosine], axis=0
    )


def project(place, inputs, weight, cut, q_cut):
    rows, width = inputs[0].shape
    kv_cut = cut - q_cut
    parcel = q_cut + DEPTHS * kv_cut

    def kernel(place_ref, *refs):
        ins, weight_ref = refs[:8], refs[8]
        hidden_ref, gains_ref = refs[9], refs[10]
        outs = refs[11:]
        depth = place_ref[1]
        pick = lax.broadcasted_iota(jnp.int32, (8, 128), 1) == (
            lax.broadcasted_iota(jnp.int32, (8, 128), 0) + (cut - 128)
        )
        gains = dot_nt(pick.astype(F32).astype(BF), weight_ref[:, 128:256])
        gains_ref[...] = gains
        gain = gains[0:1]
        for index in range(8):
            side, step = index // DEPTHS, index % DEPTHS
            value = ins[index][...].astype(F32)
            factor = lax.rsqrt(jnp.mean(value * value, axis=-1, keepdims=True) + EPS)
            hidden = (value * factor * gain).astype(BF)
            hidden_ref[index] = hidden
            block = jnp.transpose(dot(hidden, weight_ref[:, :256])).astype(BF)
            outs[step][side, :q_cut] = block[:q_cut]
            at = (depth + STEPS[step]) % DEPTHS
            at = pl.multiple_of(q_cut + kv_cut * at, 16)
            for out in outs:
                out[side, pl.ds(at, kv_cut)] = block[q_cut:cut]

    return run(
        kernel,
        [((8, rows, width), BF), ((8, width), F32)] + [((2, parcel, rows), BF)] * DEPTHS,
        list(inputs) + [weight],
        place,
        flops=2 * 8 * rows * width * 256,
    )


def attend(place, mine, theirs, cosine, sine, q_cut, k_cut):
    parcel, rows = mine[0].shape[1:]
    heads = RANKS * q_cut // HEAD
    heads_kv = RANKS * k_cut // HEAD
    keys = DEPTHS * rows
    group = heads // heads_kv
    per_side = heads // 2

    def kernel(place_ref, *refs):
        ins = refs[:8]
        cosine_ref, sine_ref = refs[8], refs[9]
        query_ref, key_ref, value_ref, stat_ref, mixed_ref = refs[10:15]
        core, depth = place_ref[0], place_ref[1]
        for index in range(8):
            side, step = index // DEPTHS, index % DEPTHS
            rank = side * DEPTHS + (depth + STEPS[step]) % DEPTHS
            block = ins[index]
            query_ref[pl.ds(pl.multiple_of(rank * q_cut, 16), q_cut)] = block[0, :q_cut]
            at = pl.ds(pl.multiple_of(rank * k_cut, 16), k_cut)
            for part in range(DEPTHS):
                low = q_cut + 2 * k_cut * part
                lanes = slice(part * rows, (part + 1) * rows)
                key_ref[at, lanes] = block[0, low : low + k_cut]
                value_ref[at, lanes] = block[0, low + k_cut : low + 2 * k_cut]
        here = pl.ds(pl.multiple_of(depth * rows, rows), rows)
        own_cosine, own_sine = cosine_ref[:, here], sine_ref[:, here]
        for head in range(heads):
            at = slice(head * HEAD, (head + 1) * HEAD)
            query_ref[at] = turned(query_ref[at].astype(F32), own_cosine, own_sine).astype(BF)
        all_cosine, all_sine = cosine_ref[...], sine_ref[...]
        for head in range(heads_kv):
            at = slice(head * HEAD, (head + 1) * HEAD)
            key_ref[at] = turned(key_ref[at].astype(F32), all_cosine, all_sine).astype(BF)
        allowed = mask_of(place_ref, rows, keys)
        lane = lax.broadcasted_iota(jnp.int32, (rows, 128), 1)
        stats = jnp.zeros((rows, 128), F32)
        for head in range(heads):
            kv = slice(head // group * HEAD, (head // group + 1) * HEAD)
            query = query_ref[head * HEAD : (head + 1) * HEAD]
            scores = dot_tn(query, key_ref[kv]) * HEAD ** (-0.5)
            scores = jnp.where(allowed, scores, -1e30)
            peak = jnp.max(scores, axis=-1, keepdims=True)
            weights = jnp.exp(scores - peak)
            total = jnp.sum(weights, axis=-1, keepdims=True)
            weights = (weights * (1.0 / total)).astype(BF)
            stats = jnp.where(lane == head, peak + jnp.log(total), stats)
            mixed = dot_nt(value_ref[kv], weights).astype(BF)
            side = head // per_side
            where = core if side == 0 else 1 - core
            at = where * (per_side * HEAD) + head % per_side * HEAD
            mixed_ref[pl.ds(pl.multiple_of(at, 16), HEAD)] = mixed
        stat_ref[...] = stats

    return run(
        kernel,
        [
            ((heads * HEAD, rows), BF),
            ((heads_kv * HEAD, keys), BF),
            ((heads_kv * HEAD, keys), BF),
            ((rows, 128), F32),
            ((heads * HEAD, rows), BF),
        ],
        list(mine) + list(theirs) + [cosine, sine],
        place,
        flops=4 * heads * rows * keys * HEAD,
        vmem=58,
        fetch=True,
        read=halves(4, 0, (parcel, rows))
        + halves(4, 1, (parcel, rows))
        + [pl.BlockSpec(cosine.shape, lambda i: (0, 0))] * 2,
    )


def mask_of(place_ref, rows, keys):
    here = place_ref[1] * rows
    row = lax.broadcasted_iota(jnp.int32, (rows, 1), 0) + here
    key = lax.broadcasted_iota(jnp.int32, (1, keys), 1)
    row_start, key_start = jnp.zeros_like(row), jnp.zeros_like(key)
    for index in range(2, 6):
        start = place_ref[index]
        row_start = jnp.maximum(row_start, jnp.where(row >= start, start, 0))
        key_start = jnp.maximum(key_start, jnp.where(key >= start, start, 0))
    return (row_start == key_start) & (key <= row)


def attend_back(place, query, key, value, stats, grad_mixed, cosine, sine, q_cut, k_cut):
    rows, keys = query.shape[1], key.shape[1]
    heads, heads_kv = query.shape[0] // HEAD, key.shape[0] // HEAD
    group = heads // heads_kv
    per_side = heads // 2
    scale = HEAD ** (-0.5)
    parcel = q_cut + 2 * DEPTHS * k_cut

    def kernel(place_ref, q_ref, k_ref, v_ref, stat_ref, grad_ref, cosine_ref, sine_ref, *refs):
        outs, (dq_ref, dk_ref, dv_ref) = refs[:DEPTHS], refs[DEPTHS:]
        core, depth = place_ref[0], place_ref[1]
        here = pl.ds(pl.multiple_of(depth * rows, rows), rows)
        own_cosine, own_sine = cosine_ref[:, here], -sine_ref[:, here]
        all_cosine, all_sine = cosine_ref[...], -sine_ref[...]
        allowed = mask_of(place_ref, rows, keys)
        for kv_head in range(heads_kv):
            kv = slice(kv_head * HEAD, (kv_head + 1) * HEAD)
            grad_key = jnp.zeros((HEAD, keys), F32)
            grad_value = jnp.zeros((HEAD, keys), F32)
            for head in range(kv_head * group, (kv_head + 1) * group):
                at = slice(head * HEAD, (head + 1) * HEAD)
                where = core if head < per_side else 1 - core
                low = where * (per_side * HEAD) + head % per_side * HEAD
                grad = grad_ref[pl.ds(pl.multiple_of(low, 16), HEAD)]
                scores = dot_tn(q_ref[at], k_ref[kv]) * scale
                scores = jnp.where(allowed, scores, -1e30)
                weights = jnp.exp(scores - stat_ref[:, head : head + 1])
                grad_weights = dot_tn(grad, v_ref[kv])
                centre = jnp.sum(weights * grad_weights, axis=-1, keepdims=True)
                grad_scores = (weights * (grad_weights - centre)).astype(BF)
                grad_query = dot_nt(k_ref[kv], grad_scores) * scale
                dq_ref[at] = turned(grad_query, own_cosine, own_sine).astype(BF)
                grad_key += dot(q_ref[at], grad_scores)
                grad_value += dot(grad, weights.astype(BF))
            dk_ref[kv] = turned(grad_key * scale, all_cosine, all_sine).astype(BF)
            dv_ref[kv] = grad_value.astype(BF)
        for index in range(8):
            side, step = index // DEPTHS, index % DEPTHS
            rank = side * DEPTHS + (depth + STEPS[step]) % DEPTHS
            out = outs[step]
            out[side, :q_cut] = dq_ref[pl.ds(pl.multiple_of(rank * q_cut, 16), q_cut)]
            at = pl.ds(pl.multiple_of(rank * k_cut, 16), k_cut)
            for part in range(DEPTHS):
                low = q_cut + 2 * k_cut * part
                lanes = slice(part * rows, (part + 1) * rows)
                out[side, low : low + k_cut] = dk_ref[at, lanes]
                out[side, low + k_cut : low + 2 * k_cut] = dv_ref[at, lanes]

    return run(
        kernel,
        [((2, parcel, rows), BF)] * DEPTHS,
        [query, key, value, stats, grad_mixed, cosine, sine],
        place,
        scratch=[
            pltpu.VMEM(query.shape, BF),
            pltpu.VMEM(key.shape, BF),
            pltpu.VMEM(key.shape, BF),
        ],
        flops=10 * heads * rows * keys * HEAD,
    )


def project_back(place, mine, theirs, hidden, parcel_in, q_cut, k_cut):
    parcel, rows = mine[0].shape[1:]
    width = hidden.shape[2]
    kv_cut = 2 * k_cut
    cut = q_cut + kv_cut
    block_rows = width // PLANES

    def kernel(place_ref, *refs):
        ins = refs[:8]
        hidden_home, parcel_ref, rows_ref, out_ref, hidden_ref, done = refs[8:]
        fetch = pltpu.make_async_copy(hidden_home, hidden_ref, done)
        fetch.start()
        out_ref[:, :, 256:] = parcel_ref[...]
        depth = place_ref[1]
        for index in range(8):
            side, step = index // DEPTHS, index % DEPTHS
            at = pl.multiple_of(q_cut + kv_cut * ((depth + STEPS[step]) % DEPTHS), 16)
            kv = sum(
                ins[side * DEPTHS + other][0, pl.ds(at, kv_cut)].astype(F32)
                for other in range(DEPTHS)
            )
            block = jnp.concatenate(
                [ins[index][0, :q_cut].astype(F32), kv, jnp.zeros((256 - cut, rows), F32)], axis=0
            )
            rows_ref[index] = jnp.transpose(block).astype(BF)
        fetch.wait()
        grad = dot_tn(hidden_ref[...].reshape(-1, width), rows_ref[...].reshape(-1, 256))
        out_ref[:, :, :256] = grad.astype(BF).reshape(PLANES, block_rows, 256)

    return run(
        kernel,
        [((8, rows, 256), BF), ((PLANES, block_rows, 256 + parcel_in.shape[2]), BF)],
        list(mine) + list(theirs) + [hidden, parcel_in],
        place,
        flops=2 * 8 * rows * width * 256,
        read=halves(4, 0, (parcel, rows))
        + halves(4, 1, (parcel, rows))
        + [AWAY, WHOLE],
        scratch=[pltpu.VMEM(hidden.shape, BF), pltpu.SemaphoreType.DMA],
    )


def side_product(left, right):
    rows, width = left.shape[1], right.shape[0]

    def kernel(left_ref, right_ref, own_ref, other_ref):
        own = dot_nt(left_ref[:DEPTHS].reshape(DEPTHS * rows, -1), right_ref[:, :256])
        own_ref[...] = own.reshape(DEPTHS, rows, width)
        other = dot_nt(left_ref[DEPTHS:].reshape(DEPTHS * rows, -1), right_ref[:, :256])
        other_ref[...] = other.astype(BF).reshape(DEPTHS, rows, width)

    return run(
        kernel,
        [((DEPTHS, rows, width), F32), ((DEPTHS, rows, width), BF)],
        [left, right],
        flops=2 * left.size * width,
    )


def side_outputs(own, other, weight):
    rows, width = own.shape[0] // DEPTHS, weight.shape[1]

    def kernel(own_in, other_in, weight_ref, own_ref, other_ref):
        own_ref[...] = dot(own_in[...], weight_ref[...]).reshape(DEPTHS, rows, width)
        other_ref[...] = dot(other_in[...], weight_ref[...]).astype(BF).reshape(DEPTHS, rows, width)

    return run(
        kernel,
        [((DEPTHS, rows, width), F32), ((DEPTHS, rows, width), BF)],
        [own, other, weight],
        flops=4 * own.size * width,
    )


def feed_forward(hidden, upstream, weight, down, kind):
    rows, width = hidden[0].shape
    inner_width = down.shape[0]

    def kernel(*refs):
        ins, ups = refs[:DEPTHS], refs[DEPTHS : 2 * DEPTHS]
        weight_ref, down_ref, inner_ref, grad_ref, out_ref = refs[2 * DEPTHS : 2 * DEPTHS + 5]
        rows_ref, expanded_ref, back_ref = refs[2 * DEPTHS + 5 :]
        for block in range(DEPTHS):
            at = slice(block * rows, (block + 1) * rows)
            rows_ref[at] = ins[block][...]
        expanded_ref[...] = dot(rows_ref[...], weight_ref[:, : 2 * inner_width])
        for block in range(DEPTHS):
            at = slice(block * rows, (block + 1) * rows)
            rows_ref[at] = ups[block][...]
        back_ref[...] = dot_nt(rows_ref[...], down_ref[...])
        for block in range(DEPTHS):
            at = slice(block * rows, (block + 1) * rows)
            gate, up_values = expanded_ref[at, :inner_width], expanded_ref[at, inner_width:]
            gate_sigmoid = jax.nn.sigmoid(gate)
            activated = gate * gate_sigmoid
            inner_ref[at] = (activated * up_values).astype(BF)
            grad_inner = back_ref[at]
            grad_ref[at, inner_width:] = (grad_inner * activated).astype(BF)
            grad_ref[at, :inner_width] = (
                grad_inner * up_values * gate_sigmoid * (1.0 + gate * (1.0 - gate_sigmoid))
            ).astype(BF)
        partial = dot_nt(grad_ref[...], weight_ref[:, : 2 * inner_width])
        out_ref[...] = partial.astype(kind).reshape(DEPTHS, rows, width)

    return run(
        kernel,
        [
            ((DEPTHS * rows, inner_width), BF),
            ((DEPTHS * rows, 2 * inner_width), BF),
            ((DEPTHS, rows, width), kind),
        ],
        list(hidden) + list(upstream) + [weight, down],
        scratch=[
            pltpu.VMEM((DEPTHS * rows, width), BF),
            pltpu.VMEM((DEPTHS * rows, 2 * inner_width), F32),
            pltpu.VMEM((DEPTHS * rows, inner_width), F32),
        ],
        flops=10 * DEPTHS * rows * width * inner_width,
    )


def add_sides(own, received):
    rows, width = own.shape[1:]

    def kernel(own_ref, received_ref, *outs):
        for step in range(DEPTHS):
            total = own_ref[step] + received_ref[step].astype(F32)
            outs[step][...] = total.astype(outs[step].dtype)

    return run(
        kernel,
        [((rows, width), F32)] + [((rows, width), BF)] * (DEPTHS - 1),
        [own, received],
    )


def ffn_gradients(hidden, grads, inner, upstream):
    rows, width = hidden[0].shape
    expanded = grads[0].shape[1]
    inner_width = inner[0].shape[1]
    third = width // 3
    block_rows, rank_rows = width // PLANES, inner_width // PLANES

    def kernel(*refs):
        hid, ups = refs[:8], refs[8:16]
        grad_own, grad_other, inner_own, inner_other, out_ref, hidden_all, upstream_all = refs[16:]
        for index in range(8):
            at = slice(index * rows, (index + 1) * rows)
            hidden_all[at] = hid[index][...]
            upstream_all[at] = ups[index][...]
        split = DEPTHS * rows
        total = dot_tn(hidden_all[:split], grad_own[...]) + dot_tn(hidden_all[split:], grad_other[...])
        out_ref[:, :, :expanded] = total.astype(BF).reshape(PLANES, block_rows, expanded)
        total = dot_tn(inner_own[...], upstream_all[:split]) + dot_tn(
            inner_other[...], upstream_all[split:]
        )
        total = total.astype(BF).reshape(PLANES, rank_rows, width)
        for part in range(3):
            out_ref[:, part * rank_rows : (part + 1) * rank_rows, expanded:] = total[
                :, :, part * third : (part + 1) * third
            ]

    return run(
        kernel,
        [((PLANES, block_rows, expanded + third), BF)],
        list(hidden) + list(upstream) + list(grads) + list(inner),
        scratch=[pltpu.VMEM((8 * rows, width), BF)] * 2,
        flops=2 * 8 * rows * width * (expanded + inner_width),
    )[0]


def into_residual(place, mixed, tokens, own_half, other_half, gains):
    half = tokens.shape[1] // 2

    def kernel(place_ref, mixed_ref, tokens_ref, own_ref, other_ref, gains_ref, residual_ref, hidden_ref):
        first = place_ref[0] == 0
        own = dot_tn(mixed_ref[...], own_ref[...])[:, :half]
        other = dot_tn(mixed_ref[...], other_ref[...])[:, :half]
        added = jnp.concatenate(
            [jnp.where(first, own, other), jnp.where(first, other, own)], axis=1
        )
        residual = tokens_ref[...].astype(F32) + added
        residual_ref[...] = residual
        factor = lax.rsqrt(jnp.mean(residual * residual, axis=-1, keepdims=True) + EPS)
        hidden_ref[...] = (residual * factor * gains_ref[1:2]).astype(BF)

    return run(
        kernel,
        [(tokens.shape, F32), (tokens.shape, BF)],
        [mixed, tokens, own_half, other_half, gains],
        place,
        flops=2 * tokens.size * mixed.shape[0],
    )


def residual_back(place, parts, residual, upstream, own_half, other_half, gains):
    rows, width = residual.shape
    half, padded = width // 2, own_half.shape[1]

    def kernel(place_ref, *refs):
        ins = refs[:DEPTHS]
        residual_ref, upstream_ref, own_ref, other_ref, gains_ref = refs[DEPTHS : DEPTHS + 5]
        grad_ref, low_ref, mixed_ref = refs[DEPTHS + 5 :]
        grad = sum(part[...].astype(F32) for part in ins) * gains_ref[1:2]
        value = residual_ref[...]
        factor = lax.rsqrt(jnp.mean(value * value, axis=-1, keepdims=True) + EPS)
        grad = upstream_ref[...].astype(F32) + norm_back(grad, value * factor, factor)
        grad_ref[...] = grad
        low_ref[...] = grad.astype(BF)
        first = place_ref[0] == 0
        left, right = grad[:, :half], grad[:, half:]
        spare = jnp.zeros((rows, padded - half), F32)
        own = jnp.concatenate([jnp.where(first, left, right), spare], axis=1).astype(BF)
        other = jnp.concatenate([jnp.where(first, right, left), spare], axis=1).astype(BF)
        mixed = dot_nt(own_ref[...], own) + dot_nt(other_ref[...], other)
        mixed_ref[...] = mixed.astype(BF)

    return run(
        kernel,
        [(residual.shape, F32), (residual.shape, BF), ((own_half.shape[0], rows), BF)],
        list(parts) + [residual, upstream, own_half, other_half, gains],
        place,
        flops=2 * residual.size * own_half.shape[0],
    )


def inputs_back(parts, tokens, grad_residual, gains):
    def kernel(*refs):
        ins = refs[:DEPTHS]
        tokens_ref, residual_ref, gains_ref, out_ref = refs[DEPTHS:]
        grad = sum(part[...].astype(F32) for part in ins) * gains_ref[0:1]
        value = tokens_ref[...].astype(F32)
        factor = lax.rsqrt(jnp.mean(value * value, axis=-1, keepdims=True) + EPS)
        out_ref[...] = residual_ref[...] + norm_back(grad, value * factor, factor)

    return run(
        kernel, [(grad_residual.shape, F32)], list(parts) + [tokens, grad_residual, gains]
    )[0]


def output_gradient(place, mixed, mixed_other, low, low_other, padded):
    rows, width = low.shape
    half = width // 2

    def kernel(place_ref, mixed_ref, mixed_other_ref, low_ref, low_other_ref, out_ref):
        first = place_ref[0] == 0
        spare = jnp.zeros((rows, padded - half), F32)
        total = 0.0
        for heads_ref, grad_ref in ((mixed_ref, low_ref), (mixed_other_ref, low_other_ref)):
            grad = grad_ref[...].astype(F32)
            grad = jnp.where(first, grad[:, :half], grad[:, half:])
            grad = jnp.concatenate([grad, spare], axis=1).astype(BF)
            total = total + dot(heads_ref[...], grad)
        out_ref[...] = total.astype(BF).reshape(PLANES, -1, padded)

    return run(
        kernel,
        [((PLANES, mixed.shape[0] // PLANES, padded), BF)],
        [mixed, mixed_other, low, low_other],
        place,
        flops=2 * mixed.size * width,
    )[0]


BLOCKS = 13


def as_column(row, count):
    one = lax.broadcasted_iota(jnp.int32, (count, count), 0)
    other = lax.broadcasted_iota(jnp.int32, (count, count), 1)
    return jnp.sum(jnp.where(one == other, row, 0.0), axis=1, keepdims=True)


def packed(blocks):
    rows = sum(block.shape[0] for block in blocks)
    spare = jnp.zeros((-rows % 8, 128), F32)
    return jnp.concatenate(list(blocks) + [spare], axis=0).astype(BF)


def prepare(segments, source, first_gain, second_gain, query, key, value, output, gate, up):
    own, width = query.shape
    q_cut, k_cut = width // RANKS, key.shape[1] // RANKS
    rank_cut = gate.shape[1] // RANKS
    piece = rank_cut // PLANES
    half = width // 2

    values = [segments, source, first_gain, second_gain, query, key, value, output, gate, up]

    def kernel(seg_ref, src_ref, one_ref, two_ref, q_ref, k_ref, v_ref, o_ref, g_ref, u_ref, out_ref):
        lane = lax.broadcasted_iota(jnp.int32, (own, 16), 1)
        tail = jnp.where(
            lane == 0,
            as_column(one_ref[...].astype(F32), own),
            jnp.where(lane == 1, as_column(two_ref[...].astype(F32), own), 0.0),
        )
        slot = lax.broadcasted_iota(jnp.int32, (1, seg_ref.shape[1]), 1)
        for buffer in range(2):
            src = src_ref[buffer : buffer + 1]
            full = (seg_ref[buffer : buffer + 1] != -1).astype(jnp.int32)
            filled = jnp.sum(full, axis=1, keepdims=True)
            at_first = jnp.sum(jnp.where(slot == 0, src, 0), axis=1, keepdims=True)
            at_pad = jnp.sum(jnp.where(slot == filled, src, 0), axis=1, keepdims=True)
            marks = (filled, at_first >> 1, at_first & 1, at_pad >> 1, at_pad & 1)
            for index, mark in enumerate(marks):
                tail = jnp.where(lane == 2 + 2 * index + buffer, mark.astype(F32), tail)
        q, k, v = q_ref[...].astype(F32), k_ref[...].astype(F32), v_ref[...].astype(F32)
        o, g, u = o_ref[...].astype(F32), g_ref[...].astype(F32), u_ref[...].astype(F32)
        sides = []
        for side in range(2):
            padded = jnp.concatenate(
                [o[:, side * half : (side + 1) * half], jnp.zeros((own, 64), F32)], axis=1
            )
            sides.append([padded[:, 128 * i : 128 * (i + 1)] for i in range(5)])
        for rank in range(RANKS):
            blocks = [
                q[:, q_cut * rank : q_cut * rank + 128],
                jnp.concatenate(
                    [
                        q[:, q_cut * rank + 128 : q_cut * (rank + 1)],
                        k[:, k_cut * rank : k_cut * (rank + 1)],
                        v[:, k_cut * rank : k_cut * (rank + 1)],
                        tail,
                    ],
                    axis=1,
                ),
            ]
            for weight in (g, u):
                cut = jnp.concatenate(
                    [
                        weight[:, low : low + piece]
                        for low in range(piece * rank, RANKS * rank_cut, RANKS * piece)
                    ],
                    axis=1,
                )
                blocks += [cut[:, 128 * i : 128 * (i + 1)] for i in range(rank_cut // 128)]
            out_ref[rank] = packed(blocks + sides[rank // DEPTHS])

    rows = own * BLOCKS
    return run(
        kernel,
        [((RANKS, rows + -rows % 8, 128), BF)],
        values,
        vmem=60,
        fetch=True,
    )[0]


def assemble(column, own, blocks, down=None):
    wide = 128 * len(blocks)
    third = 0 if down is None else down.shape[1] // 3
    rows = RANKS * own

    def kernel(column_ref, *refs):
        out_ref = refs[-1]
        parts = []
        for block in blocks:
            parts.append(
                jnp.concatenate(
                    [
                        column_ref[rank, block * own : (block + 1) * own].astype(F32)
                        for rank in range(RANKS)
                    ],
                    axis=0,
                ).astype(BF)
            )
        if down is not None:
            parts.append(
                jnp.concatenate(
                    [refs[0][:, third * i : third * (i + 1)] for i in range(3)], axis=0
                )
            )
        whole = jnp.concatenate(parts, axis=1)
        for plane in range(PLANES):
            out_ref[plane] = whole

    return run(
        kernel,
        [((PLANES, rows, wide + third), BF)],
        [column] if down is None else [column, down],
    )[0]


def unpack_down(gathered, rank_rows, wide):
    planes, rows, columns = gathered.shape
    third = columns - wide

    def kernel(in_ref, out_ref):
        for plane in range(planes):
            for part in range(3):
                out_ref[
                    plane * rank_rows : (plane + 1) * rank_rows, third * part : third * (part + 1)
                ] = in_ref[plane, part * rank_rows : (part + 1) * rank_rows, wide:]

    return run(kernel, [((planes * rank_rows, 3 * third), BF)], [gathered])[0]


def sum_ffn(received, rank_rows, wide):
    planes, rows, columns = received.shape
    third = columns - wide

    def kernel(in_ref, sum_ref, down_ref):
        total = in_ref[0].astype(F32)
        for plane in range(1, planes):
            total = total + in_ref[plane].astype(F32)
        sum_ref[...] = total[:, :wide]
        for part in range(3):
            down_ref[:, third * part : third * (part + 1)] = total[
                part * rank_rows : (part + 1) * rank_rows, wide:
            ]

    return run(kernel, [((rows, wide), F32), ((rank_rows, 3 * third), F32)], [received])


def send_sums(attention, ffn, own):
    def kernel(attention_ref, ffn_ref, out_ref):
        total = attention_ref[0].astype(F32)
        for plane in range(1, PLANES):
            total = total + attention_ref[plane].astype(F32)
        wholes = [total[:, :256], ffn_ref[...], total[:, 256:]]
        for rank in range(RANKS):
            at = slice(rank * own, (rank + 1) * own)
            out_ref[rank] = packed(
                [
                    whole[at, 128 * i : 128 * (i + 1)]
                    for whole in wholes
                    for i in range(whole.shape[1] // 128)
                ]
            )

    rows = own * BLOCKS
    return run(
        kernel, [((RANKS, rows + -rows % 8, 128), BF)], [attention, ffn]
    )[0]


def finish(received, first_gain, second_gain, query, key, value, gate, up):
    own, width = query.shape
    q_cut, k_cut = width // RANKS, key.shape[1] // RANKS
    rank_cut = gate.shape[1] // RANKS
    piece = rank_cut // PLANES
    half = width // 2

    def kernel(in_ref, one_ref, two_ref, q_in, k_in, v_in, g_in, u_in, *outs):
        one_out, q_out, k_out, v_out, o_out, two_out, g_out, u_out = outs

        def block(rank, index):
            return in_ref[rank, index * own : (index + 1) * own].astype(F32)

        second = [block(rank, 1) for rank in range(RANKS)]
        q_parts = []
        for rank in range(RANKS):
            q_parts += [block(rank, 0), second[rank][:, : q_cut - 128]]
        low = q_cut - 128
        q = jnp.concatenate(q_parts, axis=1)
        k = jnp.concatenate([part[:, low : low + k_cut] for part in second], axis=1)
        v = jnp.concatenate([part[:, low + k_cut : low + 2 * k_cut] for part in second], axis=1)
        q_out[...], k_out[...], v_out[...] = q, k, v
        ffn = []
        for base in (2, 2 + rank_cut // 128):
            wide = [
                jnp.concatenate([block(rank, base + i) for i in range(rank_cut // 128)], axis=1)
                for rank in range(RANKS)
            ]
            ffn.append(
                jnp.concatenate(
                    [
                        wide[rank][:, piece * plane : piece * (plane + 1)]
                        for plane in range(PLANES)
                        for rank in range(RANKS)
                    ],
                    axis=1,
                )
            )
        g_out[...], u_out[...] = ffn
        base = 2 + 2 * rank_cut // 128
        sides = []
        for side in range(2):
            parts = []
            for i in range(base, BLOCKS):
                total = block(side * DEPTHS, i)
                for step in range(1, DEPTHS):
                    total = total + block(side * DEPTHS + step, i)
                parts.append(total)
            sides.append(jnp.concatenate(parts, axis=1)[:, :half])
        o_out[...] = jnp.concatenate(sides, axis=1)

        def along(pairs):
            return sum(
                jnp.sum(grad * ref[...].astype(F32), axis=1, keepdims=True) for grad, ref in pairs
            )

        def as_row(column):
            rows = lax.broadcasted_iota(jnp.int32, (own, own), 0)
            columns = lax.broadcasted_iota(jnp.int32, (own, own), 1)
            return jnp.sum(jnp.where(rows == columns, column, 0.0), axis=0, keepdims=True)

        one_out[...] = as_row(along([(q, q_in), (k, k_in), (v, v_in)])) / one_ref[...].astype(F32)
        two_out[...] = as_row(along([(ffn[0], g_in), (ffn[1], u_in)])) / two_ref[...].astype(F32)

    return run(
        kernel,
        [
            ((1, own), F32),
            (query.shape, F32),
            (key.shape, F32),
            (value.shape, F32),
            (query.shape, F32),
            ((1, own), F32),
            (gate.shape, F32),
            (up.shape, F32),
        ],
        [received, first_gain, second_gain, query, key, value, gate, up],
    )


def norm_back(grad, normed, scale):
    return scale * (grad - normed * jnp.mean(grad * normed, axis=-1, keepdims=True))


def on_device(
    tokens,
    cotangent,
    segments,
    slot_source,
    first_gain,
    query_weight,
    key_projection,
    value_projection,
    output_weight,
    second_gain,
    gate_weight,
    up_weight,
    down_weight,
):
    core, depth = lax.axis_index("c"), lax.axis_index("z")
    rows, width = tokens.shape
    own = query_weight.shape[0]
    q_cut, k_cut = query_weight.shape[1] // RANKS, key_projection.shape[1] // RANKS
    rank_rows = down_weight.shape[0]
    wide = 2 * gate_weight.shape[1] // RANKS
    cut = q_cut + 2 * k_cut
    gain_one, gain_two = first_gain.reshape(1, own), second_gain.reshape(1, own)

    def column_blocks(value):
        mine = gather_depths(value)
        return mine, [exchange(block) for block in mine]

    def parcels_between(parcels):
        mine = scatter_depths(parcels)
        return mine, [exchange(block) for block in mine]

    inputs_mine, inputs_theirs = column_blocks(tokens)
    column = deal(
        prepare(
            segments[0],
            slot_source[0],
            gain_one,
            gain_two,
            query_weight,
            key_projection,
            value_projection,
            output_weight,
            gate_weight,
            up_weight,
        ),
        COLUMN,
    )
    attention_w = deal(assemble(column, own, range(2)), PLANE).reshape(width, -1)
    output_in = assemble(column, own, range(8, BLOCKS))
    ffn_in = assemble(column, own, range(2, 8), down_weight)

    marks = column.reshape(2, DEPTHS, -1, 128)[:, :, own, cut + 2 - 128 : cut + 12 - 128]
    marks = marks.astype(jnp.int32)
    marks = jnp.where(core == 0, marks[0], marks[1]).reshape(DEPTHS, 5, 2)
    padded = marks[:, 0] < segments.shape[2]
    earlier_padded = jnp.concatenate([jnp.zeros((1, 2), bool), padded[:-1]])
    pad_starts = jnp.sum(
        jnp.where(padded & ~earlier_padded, marks[:, 3] * 2 + marks[:, 4], 0), axis=0
    )
    starts = jnp.concatenate([marks[0, 1] * 2 + marks[0, 2], pad_starts])
    group_rows = jnp.arange(DEPTHS * rows)
    run_start = jnp.max(
        jnp.where(starts[None, :] <= group_rows[:, None], starts[None, :], 0), axis=1
    )
    frequency = THETA ** (-(jnp.arange(HEAD // 2).astype(F32) * 2.0 / HEAD))
    angles = frequency[:, None] * (group_rows - run_start).astype(F32)[None, :]
    cosine, sine = jnp.cos(angles), jnp.sin(angles)
    place = jnp.concatenate([jnp.stack([core, depth]), starts]).astype(jnp.int32)

    hidden_one, gains_full, *parcels = project(
        after(place, (cosine, sine)), inputs_mine + inputs_theirs, attention_w, cut, q_cut
    )
    output_own = deal(after(output_in, parcels[0]), PLANE)
    mine, theirs = parcels_between(parcels)
    ffn_blocks = deal(after(ffn_in, (output_own, theirs)), PLANE)
    output_own = output_own.reshape(width, -1)
    output_other = exchange(output_own)
    down_w = unpack_down(ffn_blocks, rank_rows, wide)
    ffn_w = ffn_blocks.reshape(width, -1)
    query, key, value, stats, mixed = attend(place, mine, theirs, cosine, sine, q_cut, k_cut)

    residual, hidden_two = into_residual(
        place, mixed, tokens, output_own, output_other, gains_full
    )
    mixed_other = exchange(mixed)
    hidden_mine, hidden_theirs = column_blocks(after(hidden_two, mixed_other))
    upstream_mine, upstream_theirs = column_blocks(after(cotangent, hidden_mine))
    inner_theirs, grads_theirs, partial_theirs = feed_forward(
        hidden_theirs, upstream_theirs, ffn_w, down_w, BF
    )
    inner_mine, grads_mine, partial_mine = feed_forward(
        hidden_mine, upstream_mine, ffn_w, down_w, F32
    )
    ffn_grads = ffn_gradients(
        hidden_mine + hidden_theirs,
        [grads_mine, grads_theirs],
        [inner_mine, inner_theirs],
        upstream_mine + upstream_theirs,
    )
    parts = scatter_depths(add_sides(partial_mine, exchange(partial_theirs)))
    ffn_sum = deal(after(ffn_grads, parts), PLANE)
    grad_residual, residual_low, grad_mixed = residual_back(
        after(place, ffn_grads), parts, residual, cotangent, output_own, output_other, gains_full
    )

    parcels = attend_back(
        place, query, key, value, stats, grad_mixed, cosine, sine, q_cut, k_cut
    )
    mine, theirs = parcels_between(parcels)
    output_grads = output_gradient(
        place,
        mixed,
        mixed_other,
        after(residual_low, parcels[0]),
        exchange(residual_low),
        output_own.shape[1],
    )
    projected_rows, attention_grads = project_back(
        place, mine, theirs, hidden_one, output_grads, q_cut, k_cut
    )
    attention_sum = deal(after(attention_grads, ffn_sum), PLANE)
    outputs_own, outputs_other = side_outputs(
        after(inner_mine, attention_grads), inner_theirs, down_w
    )
    outputs = add_sides(outputs_own, exchange(outputs_other))
    inputs_own, inputs_other = side_product(projected_rows, attention_w)
    parts = scatter_depths(add_sides(inputs_own, exchange(inputs_other)))
    gradient_tokens = inputs_back(parts, tokens, grad_residual, gains_full)
    outputs = [outputs[0]] + [after(part, parts[1:3]) for part in outputs[1:]]
    outputs = scatter_depths(outputs)
    layer_output = (residual + sum(part.astype(F32) for part in outputs)).astype(BF)

    ffn_sum, grad_down = sum_ffn(ffn_sum, rank_rows, wide)
    received = deal(send_sums(attention_sum, ffn_sum, own), COLUMN)
    one, grad_q, grad_k, grad_v, grad_o, two, grad_g, grad_u = finish(
        received,
        gain_one,
        gain_two,
        query_weight,
        key_projection,
        value_projection,
        gate_weight,
        up_weight,
    )
    return (
        layer_output,
        gradient_tokens,
        one.reshape(own),
        grad_q,
        grad_k,
        grad_v,
        grad_o,
        two.reshape(own),
        grad_g,
        grad_u,
        grad_down,
    )


def solution(mesh):
    grid = Mesh(mesh.devices.reshape(4, 4, 2, 4), ALL)
    rows = P(ALL, None)
    flat = P(ALL)
    slots = P(("y", "x", "c"), None, "z")
    return jax.shard_map(
        on_device,
        mesh=grid,
        in_specs=(rows, rows, slots, slots, flat, rows, rows, rows, rows, flat, rows, rows, rows),
        out_specs=(rows, rows, flat, rows, rows, rows, rows, flat, rows, rows, rows),
        check_vma=False,
    )
```

```python
import jax
import jax.numpy as jnp
from jax import lax
from jax.experimental import pallas as pl
from jax.experimental.pallas import tpu as pltpu
from jax.sharding import Mesh
from jax.sharding import PartitionSpec as P

HEAD = 64
EPS = 1e-05
THETA = 10000.0
BF = jnp.bfloat16
F32 = jnp.float32
ALL = ("y", "x", "c", "z")
COLUMN = ("c", "z")
PLANE = ("y", "x")
RANKS, PLANES, DEPTHS = 8, 16, 4
PARAMS = pltpu.CompilerParams(vmem_limit_bytes=56 * 1024 * 1024)


def dot(left, right):
    return jnp.dot(left, right, preferred_element_type=F32)


def dot_nt(left, right):
    return lax.dot_general(left, right, (((1,), (1,)), ((), ())), preferred_element_type=F32)


def dot_tn(left, right):
    return lax.dot_general(left, right, (((0,), (0,)), ((), ())), preferred_element_type=F32)


def exchange(value):
    return lax.ppermute(value, "c", [(0, 1), (1, 0)])


def deal(value, axes):
    return lax.all_to_all(value, axes, 0, 0, tiled=True)


def after(value, earlier):
    return lax.optimization_barrier((value, earlier))[0]


def from_depth(value, step):
    return lax.ppermute(value, "z", [(i, (i - step) % DEPTHS) for i in range(DEPTHS)])


def gather_depths(value):
    return [value, from_depth(value, 1), from_depth(value, 3), from_depth(value, 2)]


def scatter_depths(blocks):
    return [blocks[0], from_depth(blocks[2], 1), from_depth(blocks[1], 3), from_depth(blocks[3], 2)]


STEPS = (0, 1, 3, 2)


def entire(shape):
    return pl.BlockSpec(shape, lambda i: (0,) * len(shape))


def run(
    kernel, outs, values, scalars=None, scratch=(), vmem=16, flops=0, read=None, fetch=False
):
    whole = pl.BlockSpec(memory_space=pltpu.VMEM)
    specs = [entire(value.shape) if fetch else whole for value in values] if read is None else list(read)
    if scalars is not None:
        values = [scalars] + list(values)
        specs = [pl.BlockSpec(memory_space=pltpu.SMEM)] + specs
    shapes = [jax.ShapeDtypeStruct(shape, dtype) for shape, dtype in outs]
    size = sum(v.size * v.dtype.itemsize for v in values)
    size += sum(o.size * o.dtype.itemsize for o in shapes)
    return pl.pallas_call(
        kernel,
        grid=(1,),
        in_specs=specs,
        out_specs=[entire(shape) if fetch else whole for shape, _ in outs],
        out_shape=shapes,
        scratch_shapes=list(scratch),
        compiler_params=pltpu.CompilerParams(vmem_limit_bytes=vmem * 1024 * 1024),
        cost_estimate=pl.CostEstimate(
            flops=flops, bytes_accessed=size, transcendentals=0
        ),
    )(*values)


WHOLE = pl.BlockSpec(memory_space=pltpu.VMEM)
AWAY = pl.BlockSpec(memory_space=pl.ANY)


def halves(count, which, shape):
    return [pl.BlockSpec((1,) + shape, lambda i: (which, 0, 0))] * count


def turned(value, cosine, sine):
    first, second = value[: HEAD // 2], value[HEAD // 2 :]
    return jnp.concatenate(
        [first * cosine - second * sine, first * sine + second * cosine], axis=0
    )


def project(place, inputs, weight, cut, q_cut):
    rows, width = inputs[0].shape
    kv_cut = cut - q_cut
    parcel = q_cut + DEPTHS * kv_cut

    def kernel(place_ref, *refs):
        ins, weight_ref = refs[:8], refs[8]
        hidden_ref, gains_ref = refs[9], refs[10]
        outs = refs[11:]
        depth = place_ref[1]
        pick = lax.broadcasted_iota(jnp.int32, (8, 128), 1) == (
            lax.broadcasted_iota(jnp.int32, (8, 128), 0) + (cut - 128)
        )
        gains = dot_nt(pick.astype(F32).astype(BF), weight_ref[:, 128:256])
        gains_ref[...] = gains
        gain = gains[0:1]
        for index in range(8):
            side, step = index // DEPTHS, index % DEPTHS
            value = ins[index][...].astype(F32)
            factor = lax.rsqrt(jnp.mean(value * value, axis=-1, keepdims=True) + EPS)
            hidden = (value * factor * gain).astype(BF)
            hidden_ref[index] = hidden
            block = jnp.transpose(dot(hidden, weight_ref[:, :256])).astype(BF)
            outs[step][side, :q_cut] = block[:q_cut]
            at = (depth + STEPS[step]) % DEPTHS
            at = pl.multiple_of(q_cut + kv_cut * at, 16)
            for out in outs:
                out[side, pl.ds(at, kv_cut)] = block[q_cut:cut]

    return run(
        kernel,
        [((8, rows, width), BF), ((8, width), F32)] + [((2, parcel, rows), BF)] * DEPTHS,
        list(inputs) + [weight],
        place,
        flops=2 * 8 * rows * width * 256,
    )


def attend(place, mine, theirs, cosine, sine, q_cut, k_cut):
    parcel, rows = mine[0].shape[1:]
    heads = RANKS * q_cut // HEAD
    heads_kv = RANKS * k_cut // HEAD
    keys = DEPTHS * rows
    group = heads // heads_kv
    per_side = heads // 2

    def kernel(place_ref, *refs):
        ins = refs[:8]
        cosine_ref, sine_ref = refs[8], refs[9]
        query_ref, key_ref, value_ref, stat_ref, mixed_ref = refs[10:15]
        core, depth = place_ref[0], place_ref[1]
        for index in range(8):
            side, step = index // DEPTHS, index % DEPTHS
            rank = side * DEPTHS + (depth + STEPS[step]) % DEPTHS
            block = ins[index]
            query_ref[pl.ds(pl.multiple_of(rank * q_cut, 16), q_cut)] = block[0, :q_cut]
            at = pl.ds(pl.multiple_of(rank * k_cut, 16), k_cut)
            for part in range(DEPTHS):
                low = q_cut + 2 * k_cut * part
                lanes = slice(part * rows, (part + 1) * rows)
                key_ref[at, lanes] = block[0, low : low + k_cut]
                value_ref[at, lanes] = block[0, low + k_cut : low + 2 * k_cut]
        here = pl.ds(pl.multiple_of(depth * rows, rows), rows)
        own_cosine, own_sine = cosine_ref[:, here], sine_ref[:, here]
        for head in range(heads):
            at = slice(head * HEAD, (head + 1) * HEAD)
            query_ref[at] = turned(query_ref[at].astype(F32), own_cosine, own_sine).astype(BF)
        all_cosine, all_sine = cosine_ref[...], sine_ref[...]
        for head in range(heads_kv):
            at = slice(head * HEAD, (head + 1) * HEAD)
            key_ref[at] = turned(key_ref[at].astype(F32), all_cosine, all_sine).astype(BF)
        allowed = mask_of(place_ref, rows, keys)
        lane = lax.broadcasted_iota(jnp.int32, (rows, 128), 1)
        stats = jnp.zeros((rows, 128), F32)
        for head in range(heads):
            kv = slice(head // group * HEAD, (head // group + 1) * HEAD)
            query = query_ref[head * HEAD : (head + 1) * HEAD]
            scores = dot_tn(query, key_ref[kv]) * HEAD ** (-0.5)
            scores = jnp.where(allowed, scores, -1e30)
            peak = jnp.max(scores, axis=-1, keepdims=True)
            weights = jnp.exp(scores - peak)
            total = jnp.sum(weights, axis=-1, keepdims=True)
            weights = (weights * (1.0 / total)).astype(BF)
            stats = jnp.where(lane == head, peak + jnp.log(total), stats)
            mixed = dot_nt(value_ref[kv], weights).astype(BF)
            side = head // per_side
            where = core if side == 0 else 1 - core
            at = where * (per_side * HEAD) + head % per_side * HEAD
            mixed_ref[pl.ds(pl.multiple_of(at, 16), HEAD)] = mixed
        stat_ref[...] = stats

    return run(
        kernel,
        [
            ((heads * HEAD, rows), BF),
            ((heads_kv * HEAD, keys), BF),
            ((heads_kv * HEAD, keys), BF),
            ((rows, 128), F32),
            ((heads * HEAD, rows), BF),
        ],
        list(mine) + list(theirs) + [cosine, sine],
        place,
        flops=4 * heads * rows * keys * HEAD,
        vmem=58,
        fetch=True,
        read=halves(4, 0, (parcel, rows))
        + halves(4, 1, (parcel, rows))
        + [pl.BlockSpec(cosine.shape, lambda i: (0, 0))] * 2,
    )


def mask_of(place_ref, rows, keys):
    here = place_ref[1] * rows
    row = lax.broadcasted_iota(jnp.int32, (rows, 1), 0) + here
    key = lax.broadcasted_iota(jnp.int32, (1, keys), 1)
    row_start, key_start = jnp.zeros_like(row), jnp.zeros_like(key)
    for index in range(2, 6):
        start = place_ref[index]
        row_start = jnp.maximum(row_start, jnp.where(row >= start, start, 0))
        key_start = jnp.maximum(key_start, jnp.where(key >= start, start, 0))
    return (row_start == key_start) & (key <= row)


def attend_back(place, query, key, value, stats, grad_mixed, cosine, sine, q_cut, k_cut):
    rows, keys = query.shape[1], key.shape[1]
    heads, heads_kv = query.shape[0] // HEAD, key.shape[0] // HEAD
    group = heads // heads_kv
    per_side = heads // 2
    scale = HEAD ** (-0.5)
    parcel = q_cut + 2 * DEPTHS * k_cut

    def kernel(place_ref, q_ref, k_ref, v_ref, stat_ref, grad_ref, cosine_ref, sine_ref, *refs):
        outs, (dq_ref, dk_ref, dv_ref) = refs[:DEPTHS], refs[DEPTHS:]
        core, depth = place_ref[0], place_ref[1]
        here = pl.ds(pl.multiple_of(depth * rows, rows), rows)
        own_cosine, own_sine = cosine_ref[:, here], -sine_ref[:, here]
        all_cosine, all_sine = cosine_ref[...], -sine_ref[...]
        allowed = mask_of(place_ref, rows, keys)
        for kv_head in range(heads_kv):
            kv = slice(kv_head * HEAD, (kv_head + 1) * HEAD)
            grad_key = jnp.zeros((HEAD, keys), F32)
            grad_value = jnp.zeros((HEAD, keys), F32)
            for head in range(kv_head * group, (kv_head + 1) * group):
                at = slice(head * HEAD, (head + 1) * HEAD)
                where = core if head < per_side else 1 - core
                low = where * (per_side * HEAD) + head % per_side * HEAD
                grad = grad_ref[pl.ds(pl.multiple_of(low, 16), HEAD)]
                scores = dot_tn(q_ref[at], k_ref[kv]) * scale
                scores = jnp.where(allowed, scores, -1e30)
                weights = jnp.exp(scores - stat_ref[:, head : head + 1])
                grad_weights = dot_tn(grad, v_ref[kv])
                centre = jnp.sum(weights * grad_weights, axis=-1, keepdims=True)
                grad_scores = (weights * (grad_weights - centre)).astype(BF)
                grad_query = dot_nt(k_ref[kv], grad_scores) * scale
                dq_ref[at] = turned(grad_query, own_cosine, own_sine).astype(BF)
                grad_key += dot(q_ref[at], grad_scores)
                grad_value += dot(grad, weights.astype(BF))
            dk_ref[kv] = turned(grad_key * scale, all_cosine, all_sine).astype(BF)
            dv_ref[kv] = grad_value.astype(BF)
        for index in range(8):
            side, step = index // DEPTHS, index % DEPTHS
            rank = side * DEPTHS + (depth + STEPS[step]) % DEPTHS
            out = outs[step]
            out[side, :q_cut] = dq_ref[pl.ds(pl.multiple_of(rank * q_cut, 16), q_cut)]
            at = pl.ds(pl.multiple_of(rank * k_cut, 16), k_cut)
            for part in range(DEPTHS):
                low = q_cut + 2 * k_cut * part
                lanes = slice(part * rows, (part + 1) * rows)
                out[side, low : low + k_cut] = dk_ref[at, lanes]
                out[side, low + k_cut : low + 2 * k_cut] = dv_ref[at, lanes]

    return run(
        kernel,
        [((2, parcel, rows), BF)] * DEPTHS,
        [query, key, value, stats, grad_mixed, cosine, sine],
        place,
        scratch=[
            pltpu.VMEM(query.shape, BF),
            pltpu.VMEM(key.shape, BF),
            pltpu.VMEM(key.shape, BF),
        ],
        flops=10 * heads * rows * keys * HEAD,
    )


def project_back(place, mine, theirs, hidden, parcel_in, q_cut, k_cut):
    parcel, rows = mine[0].shape[1:]
    width = hidden.shape[2]
    kv_cut = 2 * k_cut
    cut = q_cut + kv_cut
    block_rows = width // PLANES

    def kernel(place_ref, *refs):
        ins = refs[:8]
        hidden_home, parcel_ref, rows_ref, out_ref, hidden_ref, done = refs[8:]
        fetch = pltpu.make_async_copy(hidden_home, hidden_ref, done)
        fetch.start()
        out_ref[:, :, 256:] = parcel_ref[...]
        depth = place_ref[1]
        for index in range(8):
            side, step = index // DEPTHS, index % DEPTHS
            at = pl.multiple_of(q_cut + kv_cut * ((depth + STEPS[step]) % DEPTHS), 16)
            kv = sum(
                ins[side * DEPTHS + other][0, pl.ds(at, kv_cut)].astype(F32)
                for other in range(DEPTHS)
            )
            block = jnp.concatenate(
                [ins[index][0, :q_cut].astype(F32), kv, jnp.zeros((256 - cut, rows), F32)], axis=0
            )
            rows_ref[index] = jnp.transpose(block).astype(BF)
        fetch.wait()
        grad = dot_tn(hidden_ref[...].reshape(-1, width), rows_ref[...].reshape(-1, 256))
        out_ref[:, :, :256] = grad.astype(BF).reshape(PLANES, block_rows, 256)

    return run(
        kernel,
        [((8, rows, 256), BF), ((PLANES, block_rows, 256 + parcel_in.shape[2]), BF)],
        list(mine) + list(theirs) + [hidden, parcel_in],
        place,
        flops=2 * 8 * rows * width * 256,
        read=halves(4, 0, (parcel, rows))
        + halves(4, 1, (parcel, rows))
        + [AWAY, WHOLE],
        scratch=[pltpu.VMEM(hidden.shape, BF), pltpu.SemaphoreType.DMA],
    )


def side_product(left, right):
    rows, width = left.shape[1], right.shape[0]

    def kernel(left_ref, right_ref, own_ref, other_ref):
        own = dot_nt(left_ref[:DEPTHS].reshape(DEPTHS * rows, -1), right_ref[:, :256])
        own_ref[...] = own.reshape(DEPTHS, rows, width)
        other = dot_nt(left_ref[DEPTHS:].reshape(DEPTHS * rows, -1), right_ref[:, :256])
        other_ref[...] = other.astype(BF).reshape(DEPTHS, rows, width)

    return run(
        kernel,
        [((DEPTHS, rows, width), F32), ((DEPTHS, rows, width), BF)],
        [left, right],
        flops=2 * left.size * width,
    )


def side_outputs(own, other, weight):
    rows, width = own.shape[0] // DEPTHS, weight.shape[1]

    def kernel(own_in, other_in, weight_ref, own_ref, other_ref):
        own_ref[...] = dot(own_in[...], weight_ref[...]).reshape(DEPTHS, rows, width)
        other_ref[...] = dot(other_in[...], weight_ref[...]).astype(BF).reshape(DEPTHS, rows, width)

    return run(
        kernel,
        [((DEPTHS, rows, width), F32), ((DEPTHS, rows, width), BF)],
        [own, other, weight],
        flops=4 * own.size * width,
    )


def feed_forward(hidden, upstream, weight, down, kind):
    rows, width = hidden[0].shape
    inner_width = down.shape[0]

    def kernel(*refs):
        ins, ups = refs[:DEPTHS], refs[DEPTHS : 2 * DEPTHS]
        weight_ref, down_ref, inner_ref, grad_ref, out_ref = refs[2 * DEPTHS : 2 * DEPTHS + 5]
        rows_ref, expanded_ref, back_ref = refs[2 * DEPTHS + 5 :]
        for block in range(DEPTHS):
            at = slice(block * rows, (block + 1) * rows)
            rows_ref[at] = ins[block][...]
        expanded_ref[...] = dot(rows_ref[...], weight_ref[:, : 2 * inner_width])
        for block in range(DEPTHS):
            at = slice(block * rows, (block + 1) * rows)
            rows_ref[at] = ups[block][...]
        back_ref[...] = dot_nt(rows_ref[...], down_ref[...])
        for block in range(DEPTHS):
            at = slice(block * rows, (block + 1) * rows)
            gate, up_values = expanded_ref[at, :inner_width], expanded_ref[at, inner_width:]
            gate_sigmoid = jax.nn.sigmoid(gate)
            activated = gate * gate_sigmoid
            inner_ref[at] = (activated * up_values).astype(BF)
            grad_inner = back_ref[at]
            grad_ref[at, inner_width:] = (grad_inner * activated).astype(BF)
            grad_ref[at, :inner_width] = (
                grad_inner * up_values * gate_sigmoid * (1.0 + gate * (1.0 - gate_sigmoid))
            ).astype(BF)
        partial = dot_nt(grad_ref[...], weight_ref[:, : 2 * inner_width])
        out_ref[...] = partial.astype(kind).reshape(DEPTHS, rows, width)

    return run(
        kernel,
        [
            ((DEPTHS * rows, inner_width), BF),
            ((DEPTHS * rows, 2 * inner_width), BF),
            ((DEPTHS, rows, width), kind),
        ],
        list(hidden) + list(upstream) + [weight, down],
        scratch=[
            pltpu.VMEM((DEPTHS * rows, width), BF),
            pltpu.VMEM((DEPTHS * rows, 2 * inner_width), F32),
            pltpu.VMEM((DEPTHS * rows, inner_width), F32),
        ],
        flops=10 * DEPTHS * rows * width * inner_width,
    )


def add_sides(own, received):
    rows, width = own.shape[1:]

    def kernel(own_ref, received_ref, *outs):
        for step in range(DEPTHS):
            total = own_ref[step] + received_ref[step].astype(F32)
            outs[step][...] = total.astype(outs[step].dtype)

    return run(
        kernel,
        [((rows, width), F32)] + [((rows, width), BF)] * (DEPTHS - 1),
        [own, received],
    )


def ffn_gradients(hidden, grads, inner, upstream):
    rows, width = hidden[0].shape
    expanded = grads[0].shape[1]
    inner_width = inner[0].shape[1]
    third = width // 3
    block_rows, rank_rows = width // PLANES, inner_width // PLANES

    def kernel(*refs):
        hid, ups = refs[:8], refs[8:16]
        grad_own, grad_other, inner_own, inner_other, out_ref, hidden_all, upstream_all = refs[16:]
        for index in range(8):
            at = slice(index * rows, (index + 1) * rows)
            hidden_all[at] = hid[index][...]
            upstream_all[at] = ups[index][...]
        split = DEPTHS * rows
        total = dot_tn(hidden_all[:split], grad_own[...]) + dot_tn(hidden_all[split:], grad_other[...])
        out_ref[:, :, :expanded] = total.astype(BF).reshape(PLANES, block_rows, expanded)
        total = dot_tn(inner_own[...], upstream_all[:split]) + dot_tn(
            inner_other[...], upstream_all[split:]
        )
        total = total.astype(BF).reshape(PLANES, rank_rows, width)
        for part in range(3):
            out_ref[:, part * rank_rows : (part + 1) * rank_rows, expanded:] = total[
                :, :, part * third : (part + 1) * third
            ]

    return run(
        kernel,
        [((PLANES, block_rows, expanded + third), BF)],
        list(hidden) + list(upstream) + list(grads) + list(inner),
        scratch=[pltpu.VMEM((8 * rows, width), BF)] * 2,
        flops=2 * 8 * rows * width * (expanded + inner_width),
    )[0]


def into_residual(place, mixed, tokens, own_half, other_half, gains):
    half = tokens.shape[1] // 2

    def kernel(place_ref, mixed_ref, tokens_ref, own_ref, other_ref, gains_ref, residual_ref, hidden_ref):
        first = place_ref[0] == 0
        own = dot_tn(mixed_ref[...], own_ref[...])[:, :half]
        other = dot_tn(mixed_ref[...], other_ref[...])[:, :half]
        added = jnp.concatenate(
            [jnp.where(first, own, other), jnp.where(first, other, own)], axis=1
        )
        residual = tokens_ref[...].astype(F32) + added
        residual_ref[...] = residual
        factor = lax.rsqrt(jnp.mean(residual * residual, axis=-1, keepdims=True) + EPS)
        hidden_ref[...] = (residual * factor * gains_ref[1:2]).astype(BF)

    return run(
        kernel,
        [(tokens.shape, F32), (tokens.shape, BF)],
        [mixed, tokens, own_half, other_half, gains],
        place,
        flops=2 * tokens.size * mixed.shape[0],
    )


def residual_back(place, parts, residual, upstream, own_half, other_half, gains):
    rows, width = residual.shape
    half, padded = width // 2, own_half.shape[1]

    def kernel(place_ref, *refs):
        ins = refs[:DEPTHS]
        residual_ref, upstream_ref, own_ref, other_ref, gains_ref = refs[DEPTHS : DEPTHS + 5]
        grad_ref, low_ref, mixed_ref = refs[DEPTHS + 5 :]
        grad = sum(part[...].astype(F32) for part in ins) * gains_ref[1:2]
        value = residual_ref[...]
        factor = lax.rsqrt(jnp.mean(value * value, axis=-1, keepdims=True) + EPS)
        grad = upstream_ref[...].astype(F32) + norm_back(grad, value * factor, factor)
        grad_ref[...] = grad
        low_ref[...] = grad.astype(BF)
        first = place_ref[0] == 0
        left, right = grad[:, :half], grad[:, half:]
        spare = jnp.zeros((rows, padded - half), F32)
        own = jnp.concatenate([jnp.where(first, left, right), spare], axis=1).astype(BF)
        other = jnp.concatenate([jnp.where(first, right, left), spare], axis=1).astype(BF)
        mixed = dot_nt(own_ref[...], own) + dot_nt(other_ref[...], other)
        mixed_ref[...] = mixed.astype(BF)

    return run(
        kernel,
        [(residual.shape, F32), (residual.shape, BF), ((own_half.shape[0], rows), BF)],
        list(parts) + [residual, upstream, own_half, other_half, gains],
        place,
        flops=2 * residual.size * own_half.shape[0],
    )


def inputs_back(parts, tokens, grad_residual, gains):
    def kernel(*refs):
        ins = refs[:DEPTHS]
        tokens_ref, residual_ref, gains_ref, out_ref = refs[DEPTHS:]
        grad = sum(part[...].astype(F32) for part in ins) * gains_ref[0:1]
        value = tokens_ref[...].astype(F32)
        factor = lax.rsqrt(jnp.mean(value * value, axis=-1, keepdims=True) + EPS)
        out_ref[...] = residual_ref[...] + norm_back(grad, value * factor, factor)

    return run(
        kernel, [(grad_residual.shape, F32)], list(parts) + [tokens, grad_residual, gains]
    )[0]


def output_gradient(place, mixed, mixed_other, low, low_other, padded):
    rows, width = low.shape
    half = width // 2

    def kernel(place_ref, mixed_ref, mixed_other_ref, low_ref, low_other_ref, out_ref):
        first = place_ref[0] == 0
        spare = jnp.zeros((rows, padded - half), F32)
        total = 0.0
        for heads_ref, grad_ref in ((mixed_ref, low_ref), (mixed_other_ref, low_other_ref)):
            grad = grad_ref[...].astype(F32)
            grad = jnp.where(first, grad[:, :half], grad[:, half:])
            grad = jnp.concatenate([grad, spare], axis=1).astype(BF)
            total = total + dot(heads_ref[...], grad)
        out_ref[...] = total.astype(BF).reshape(PLANES, -1, padded)

    return run(
        kernel,
        [((PLANES, mixed.shape[0] // PLANES, padded), BF)],
        [mixed, mixed_other, low, low_other],
        place,
        flops=2 * mixed.size * width,
    )[0]


BLOCKS = 13


def as_column(row, count):
    one = lax.broadcasted_iota(jnp.int32, (count, count), 0)
    other = lax.broadcasted_iota(jnp.int32, (count, count), 1)
    return jnp.sum(jnp.where(one == other, row, 0.0), axis=1, keepdims=True)


def packed(blocks):
    rows = sum(block.shape[0] for block in blocks)
    spare = jnp.zeros((-rows % 8, 128), F32)
    return jnp.concatenate(list(blocks) + [spare], axis=0).astype(BF)


def prepare(segments, source, first_gain, second_gain, query, key, value, output, gate, up):
    own, width = query.shape
    q_cut, k_cut = width // RANKS, key.shape[1] // RANKS
    rank_cut = gate.shape[1] // RANKS
    piece = rank_cut // PLANES
    half = width // 2

    values = [segments, source, first_gain, second_gain, query, key, value, output, gate, up]

    def kernel(seg_ref, src_ref, one_ref, two_ref, q_ref, k_ref, v_ref, o_ref, g_ref, u_ref, out_ref):
        lane = lax.broadcasted_iota(jnp.int32, (own, 16), 1)
        tail = jnp.where(
            lane == 0,
            as_column(one_ref[...].astype(F32), own),
            jnp.where(lane == 1, as_column(two_ref[...].astype(F32), own), 0.0),
        )
        slot = lax.broadcasted_iota(jnp.int32, (1, seg_ref.shape[1]), 1)
        for buffer in range(2):
            src = src_ref[buffer : buffer + 1]
            full = (seg_ref[buffer : buffer + 1] != -1).astype(jnp.int32)
            filled = jnp.sum(full, axis=1, keepdims=True)
            at_first = jnp.sum(jnp.where(slot == 0, src, 0), axis=1, keepdims=True)
            at_pad = jnp.sum(jnp.where(slot == filled, src, 0), axis=1, keepdims=True)
            marks = (filled, at_first >> 1, at_first & 1, at_pad >> 1, at_pad & 1)
            for index, mark in enumerate(marks):
                tail = jnp.where(lane == 2 + 2 * index + buffer, mark.astype(F32), tail)
        q, k, v = q_ref[...].astype(F32), k_ref[...].astype(F32), v_ref[...].astype(F32)
        o, g, u = o_ref[...].astype(F32), g_ref[...].astype(F32), u_ref[...].astype(F32)
        sides = []
        for side in range(2):
            padded = jnp.concatenate(
                [o[:, side * half : (side + 1) * half], jnp.zeros((own, 64), F32)], axis=1
            )
            sides.append([padded[:, 128 * i : 128 * (i + 1)] for i in range(5)])
        for rank in range(RANKS):
            blocks = [
                q[:, q_cut * rank : q_cut * rank + 128],
                jnp.concatenate(
                    [
                        q[:, q_cut * rank + 128 : q_cut * (rank + 1)],
                        k[:, k_cut * rank : k_cut * (rank + 1)],
                        v[:, k_cut * rank : k_cut * (rank + 1)],
                        tail,
                    ],
                    axis=1,
                ),
            ]
            for weight in (g, u):
                cut = jnp.concatenate(
                    [
                        weight[:, low : low + piece]
                        for low in range(piece * rank, RANKS * rank_cut, RANKS * piece)
                    ],
                    axis=1,
                )
                blocks += [cut[:, 128 * i : 128 * (i + 1)] for i in range(rank_cut // 128)]
            out_ref[rank] = packed(blocks + sides[rank // DEPTHS])

    rows = own * BLOCKS
    return run(
        kernel,
        [((RANKS, rows + -rows % 8, 128), BF)],
        values,
        vmem=60,
        fetch=True,
    )[0]


def assemble(column, own, blocks, down=None):
    wide = 128 * len(blocks)
    third = 0 if down is None else down.shape[1] // 3
    rows = RANKS * own

    def kernel(column_ref, *refs):
        out_ref = refs[-1]
        parts = []
        for block in blocks:
            parts.append(
                jnp.concatenate(
                    [
                        column_ref[rank, block * own : (block + 1) * own].astype(F32)
                        for rank in range(RANKS)
                    ],
                    axis=0,
                ).astype(BF)
            )
        if down is not None:
            parts.append(
                jnp.concatenate(
                    [refs[0][:, third * i : third * (i + 1)] for i in range(3)], axis=0
                )
            )
        whole = jnp.concatenate(parts, axis=1)
        for plane in range(PLANES):
            out_ref[plane] = whole

    return run(
        kernel,
        [((PLANES, rows, wide + third), BF)],
        [column] if down is None else [column, down],
    )[0]


def unpack_down(gathered, rank_rows, wide):
    planes, rows, columns = gathered.shape
    third = columns - wide

    def kernel(in_ref, out_ref):
        for plane in range(planes):
            for part in range(3):
                out_ref[
                    plane * rank_rows : (plane + 1) * rank_rows, third * part : third * (part + 1)
                ] = in_ref[plane, part * rank_rows : (part + 1) * rank_rows, wide:]

    return run(kernel, [((planes * rank_rows, 3 * third), BF)], [gathered])[0]


def sum_ffn(received, rank_rows, wide):
    planes, rows, columns = received.shape
    third = columns - wide

    def kernel(in_ref, sum_ref, down_ref):
        total = in_ref[0].astype(F32)
        for plane in range(1, planes):
            total = total + in_ref[plane].astype(F32)
        sum_ref[...] = total[:, :wide]
        for part in range(3):
            down_ref[:, third * part : third * (part + 1)] = total[
                part * rank_rows : (part + 1) * rank_rows, wide:
            ]

    return run(kernel, [((rows, wide), F32), ((rank_rows, 3 * third), F32)], [received])


def send_sums(attention, ffn, own):
    def kernel(attention_ref, ffn_ref, out_ref):
        total = attention_ref[0].astype(F32)
        for plane in range(1, PLANES):
            total = total + attention_ref[plane].astype(F32)
        wholes = [total[:, :256], ffn_ref[...], total[:, 256:]]
        for rank in range(RANKS):
            at = slice(rank * own, (rank + 1) * own)
            out_ref[rank] = packed(
                [
                    whole[at, 128 * i : 128 * (i + 1)]
                    for whole in wholes
                    for i in range(whole.shape[1] // 128)
                ]
            )

    rows = own * BLOCKS
    return run(
        kernel, [((RANKS, rows + -rows % 8, 128), BF)], [attention, ffn]
    )[0]


def finish(received, first_gain, second_gain, query, key, value, gate, up):
    own, width = query.shape
    q_cut, k_cut = width // RANKS, key.shape[1] // RANKS
    rank_cut = gate.shape[1] // RANKS
    piece = rank_cut // PLANES
    half = width // 2

    def kernel(in_ref, one_ref, two_ref, q_in, k_in, v_in, g_in, u_in, *outs):
        one_out, q_out, k_out, v_out, o_out, two_out, g_out, u_out = outs

        def block(rank, index):
            return in_ref[rank, index * own : (index + 1) * own].astype(F32)

        second = [block(rank, 1) for rank in range(RANKS)]
        q_parts = []
        for rank in range(RANKS):
            q_parts += [block(rank, 0), second[rank][:, : q_cut - 128]]
        low = q_cut - 128
        q = jnp.concatenate(q_parts, axis=1)
        k = jnp.concatenate([part[:, low : low + k_cut] for part in second], axis=1)
        v = jnp.concatenate([part[:, low + k_cut : low + 2 * k_cut] for part in second], axis=1)
        q_out[...], k_out[...], v_out[...] = q, k, v
        ffn = []
        for base in (2, 2 + rank_cut // 128):
            wide = [
                jnp.concatenate([block(rank, base + i) for i in range(rank_cut // 128)], axis=1)
                for rank in range(RANKS)
            ]
            ffn.append(
                jnp.concatenate(
                    [
                        wide[rank][:, piece * plane : piece * (plane + 1)]
                        for plane in range(PLANES)
                        for rank in range(RANKS)
                    ],
                    axis=1,
                )
            )
        g_out[...], u_out[...] = ffn
        base = 2 + 2 * rank_cut // 128
        sides = []
        for side in range(2):
            parts = []
            for i in range(base, BLOCKS):
                total = block(side * DEPTHS, i)
                for step in range(1, DEPTHS):
                    total = total + block(side * DEPTHS + step, i)
                parts.append(total)
            sides.append(jnp.concatenate(parts, axis=1)[:, :half])
        o_out[...] = jnp.concatenate(sides, axis=1)

        def along(pairs):
            return sum(
                jnp.sum(grad * ref[...].astype(F32), axis=1, keepdims=True) for grad, ref in pairs
            )

        def as_row(column):
            rows = lax.broadcasted_iota(jnp.int32, (own, own), 0)
            columns = lax.broadcasted_iota(jnp.int32, (own, own), 1)
            return jnp.sum(jnp.where(rows == columns, column, 0.0), axis=0, keepdims=True)

        one_out[...] = as_row(along([(q, q_in), (k, k_in), (v, v_in)])) / one_ref[...].astype(F32)
        two_out[...] = as_row(along([(ffn[0], g_in), (ffn[1], u_in)])) / two_ref[...].astype(F32)

    return run(
        kernel,
        [
            ((1, own), F32),
            (query.shape, F32),
            (key.shape, F32),
            (value.shape, F32),
            (query.shape, F32),
            ((1, own), F32),
            (gate.shape, F32),
            (up.shape, F32),
        ],
        [received, first_gain, second_gain, query, key, value, gate, up],
    )


def norm_back(grad, normed, scale):
    return scale * (grad - normed * jnp.mean(grad * normed, axis=-1, keepdims=True))


def on_device(
    tokens,
    cotangent,
    segments,
    slot_source,
    first_gain,
    query_weight,
    key_projection,
    value_projection,
    output_weight,
    second_gain,
    gate_weight,
    up_weight,
    down_weight,
):
    core, depth = lax.axis_index("c"), lax.axis_index("z")
    rows, width = tokens.shape
    own = query_weight.shape[0]
    q_cut, k_cut = query_weight.shape[1] // RANKS, key_projection.shape[1] // RANKS
    rank_rows = down_weight.shape[0]
    wide = 2 * gate_weight.shape[1] // RANKS
    cut = q_cut + 2 * k_cut
    gain_one, gain_two = first_gain.reshape(1, own), second_gain.reshape(1, own)

    def column_blocks(value):
        mine = gather_depths(value)
        return mine, [exchange(block) for block in mine]

    def parcels_between(parcels):
        mine = scatter_depths(parcels)
        return mine, [exchange(block) for block in mine]

    inputs_mine, inputs_theirs = column_blocks(tokens)
    column = deal(
        prepare(
            segments[0],
            slot_source[0],
            gain_one,
            gain_two,
            query_weight,
            key_projection,
            value_projection,
            output_weight,
            gate_weight,
            up_weight,
        ),
        COLUMN,
    )
    attention_w = deal(assemble(column, own, range(2)), PLANE).reshape(width, -1)
    output_in = assemble(column, own, range(8, BLOCKS))
    ffn_in = assemble(column, own, range(2, 8), down_weight)

    marks = column.reshape(2, DEPTHS, -1, 128)[:, :, own, cut + 2 - 128 : cut + 12 - 128]
    marks = marks.astype(jnp.int32)
    marks = jnp.where(core == 0, marks[0], marks[1]).reshape(DEPTHS, 5, 2)
    padded = marks[:, 0] < segments.shape[2]
    earlier_padded = jnp.concatenate([jnp.zeros((1, 2), bool), padded[:-1]])
    pad_starts = jnp.sum(
        jnp.where(padded & ~earlier_padded, marks[:, 3] * 2 + marks[:, 4], 0), axis=0
    )
    starts = jnp.concatenate([marks[0, 1] * 2 + marks[0, 2], pad_starts])
    group_rows = jnp.arange(DEPTHS * rows)
    run_start = jnp.max(
        jnp.where(starts[None, :] <= group_rows[:, None], starts[None, :], 0), axis=1
    )
    frequency = THETA ** (-(jnp.arange(HEAD // 2).astype(F32) * 2.0 / HEAD))
    angles = frequency[:, None] * (group_rows - run_start).astype(F32)[None, :]
    cosine, sine = jnp.cos(angles), jnp.sin(angles)
    place = jnp.concatenate([jnp.stack([core, depth]), starts]).astype(jnp.int32)

    hidden_one, gains_full, *parcels = project(
        after(place, (cosine, sine)), inputs_mine + inputs_theirs, attention_w, cut, q_cut
    )
    output_own = deal(after(output_in, parcels[0]), PLANE)
    mine, theirs = parcels_between(parcels)
    upstream_mine = gather_depths(after(cotangent, theirs[3]))
    ffn_blocks = deal(after(ffn_in, (output_own, theirs)), PLANE)
    output_own = output_own.reshape(width, -1)
    output_other = exchange(output_own)
    down_w = unpack_down(ffn_blocks, rank_rows, wide)
    ffn_w = ffn_blocks.reshape(width, -1)
    query, key, value, stats, mixed = attend(place, mine, theirs, cosine, sine, q_cut, k_cut)

    residual, hidden_two = into_residual(
        place, mixed, tokens, output_own, output_other, gains_full
    )
    mixed_other = exchange(mixed)
    hidden_mine, hidden_theirs = column_blocks(after(hidden_two, mixed_other))
    upstream_theirs = [exchange(after(block, hidden_mine)) for block in upstream_mine]
    inner_theirs, grads_theirs, partial_theirs = feed_forward(
        hidden_theirs, upstream_theirs, ffn_w, down_w, BF
    )
    inner_mine, grads_mine, partial_mine = feed_forward(
        hidden_mine, upstream_mine, ffn_w, down_w, F32
    )
    ffn_grads = ffn_gradients(
        hidden_mine + hidden_theirs,
        [grads_mine, grads_theirs],
        [inner_mine, inner_theirs],
        upstream_mine + upstream_theirs,
    )
    parts = scatter_depths(add_sides(partial_mine, exchange(partial_theirs)))
    grad_residual, residual_low, grad_mixed = residual_back(
        after(place, ffn_grads), parts, residual, cotangent, output_own, output_other, gains_full
    )
    ffn_sum = deal(after(ffn_grads, residual_low), PLANE)

    parcels = attend_back(
        place, query, key, value, stats, grad_mixed, cosine, sine, q_cut, k_cut
    )
    mine, theirs = parcels_between(parcels)
    output_grads = output_gradient(
        place,
        mixed,
        mixed_other,
        after(residual_low, parcels[0]),
        exchange(residual_low),
        output_own.shape[1],
    )
    projected_rows, attention_grads = project_back(
        place, mine, theirs, hidden_one, output_grads, q_cut, k_cut
    )
    attention_sum = deal(after(attention_grads, ffn_sum), PLANE)
    outputs_own, outputs_other = side_outputs(
        after(inner_mine, attention_grads), inner_theirs, down_w
    )
    outputs = add_sides(outputs_own, exchange(outputs_other))
    inputs_own, inputs_other = side_product(projected_rows, attention_w)
    parts = scatter_depths(add_sides(inputs_own, exchange(inputs_other)))
    gradient_tokens = inputs_back(parts, tokens, grad_residual, gains_full)
    outputs = [outputs[0]] + [after(part, parts[1:3]) for part in outputs[1:]]
    outputs = scatter_depths(outputs)
    layer_output = (residual + sum(part.astype(F32) for part in outputs)).astype(BF)

    ffn_sum, grad_down = sum_ffn(ffn_sum, rank_rows, wide)
    received = deal(send_sums(attention_sum, ffn_sum, own), COLUMN)
    one, grad_q, grad_k, grad_v, grad_o, two, grad_g, grad_u = finish(
        received,
        gain_one,
        gain_two,
        query_weight,
        key_projection,
        value_projection,
        gate_weight,
        up_weight,
    )
    return (
        layer_output,
        gradient_tokens,
        one.reshape(own),
        grad_q,
        grad_k,
        grad_v,
        grad_o,
        two.reshape(own),
        grad_g,
        grad_u,
        grad_down,
    )


def solution(mesh):
    grid = Mesh(mesh.devices.reshape(4, 4, 2, 4), ALL)
    rows = P(ALL, None)
    flat = P(ALL)
    slots = P(("y", "x", "c"), None, "z")
    return jax.shard_map(
        on_device,
        mesh=grid,
        in_specs=(rows, rows, slots, slots, flat, rows, rows, rows, rows, flat, rows, rows, rows),
        out_specs=(rows, rows, flat, rows, rows, rows, rows, flat, rows, rows, rows),
        check_vma=False,
    )
```

```python
import jax
import jax.numpy as jnp
from jax import lax
from jax.experimental import pallas as pl
from jax.experimental.pallas import tpu as pltpu
from jax.sharding import Mesh
from jax.sharding import PartitionSpec as P

HEAD = 64
EPS = 1e-05
THETA = 10000.0
BF = jnp.bfloat16
F32 = jnp.float32
ALL = ("y", "x", "c", "z")
COLUMN = ("c", "z")
PLANE = ("y", "x")
RANKS, PLANES, DEPTHS = 8, 16, 4
PARAMS = pltpu.CompilerParams(vmem_limit_bytes=56 * 1024 * 1024)


def dot(left, right):
    return jnp.dot(left, right, preferred_element_type=F32)


def dot_nt(left, right):
    return lax.dot_general(left, right, (((1,), (1,)), ((), ())), preferred_element_type=F32)


def dot_tn(left, right):
    return lax.dot_general(left, right, (((0,), (0,)), ((), ())), preferred_element_type=F32)


def exchange(value):
    return lax.ppermute(value, "c", [(0, 1), (1, 0)])


def deal(value, axes):
    return lax.all_to_all(value, axes, 0, 0, tiled=True)


def after(value, earlier):
    return lax.optimization_barrier((value, earlier))[0]


def from_depth(value, step):
    return lax.ppermute(value, "z", [(i, (i - step) % DEPTHS) for i in range(DEPTHS)])


def gather_depths(value):
    return [value, from_depth(value, 1), from_depth(value, 3), from_depth(value, 2)]


def scatter_depths(blocks):
    return [blocks[0], from_depth(blocks[2], 1), from_depth(blocks[1], 3), from_depth(blocks[3], 2)]


STEPS = (0, 1, 3, 2)


FLOPS_PER_MICRO = 1.15e9


def entire(shape):
    return pl.BlockSpec(shape, lambda i: (0,) * len(shape))


def run(
    micros, kernel, outs, values, scalars=None, scratch=(), vmem=16, read=None, fetch=False
):
    whole = pl.BlockSpec(memory_space=pltpu.VMEM)
    specs = [entire(value.shape) if fetch else whole for value in values] if read is None else list(read)
    if scalars is not None:
        values = [scalars] + list(values)
        specs = [pl.BlockSpec(memory_space=pltpu.SMEM)] + specs
    shapes = [jax.ShapeDtypeStruct(shape, dtype) for shape, dtype in outs]
    size = sum(v.size * v.dtype.itemsize for v in values)
    size += sum(o.size * o.dtype.itemsize for o in shapes)
    return pl.pallas_call(
        kernel,
        grid=(1,),
        in_specs=specs,
        out_specs=[entire(shape) if fetch else whole for shape, _ in outs],
        out_shape=shapes,
        scratch_shapes=list(scratch),
        compiler_params=pltpu.CompilerParams(vmem_limit_bytes=vmem * 1024 * 1024),
        cost_estimate=pl.CostEstimate(
            flops=int(micros * FLOPS_PER_MICRO), bytes_accessed=size, transcendentals=0
        ),
    )(*values)


WHOLE = pl.BlockSpec(memory_space=pltpu.VMEM)
AWAY = pl.BlockSpec(memory_space=pl.ANY)


def halves(count, which, shape):
    return [pl.BlockSpec((1,) + shape, lambda i: (which, 0, 0))] * count


def turned(value, cosine, sine):
    first, second = value[: HEAD // 2], value[HEAD // 2 :]
    return jnp.concatenate(
        [first * cosine - second * sine, first * sine + second * cosine], axis=0
    )


def project(place, inputs, weight, cut, q_cut):
    rows, width = inputs[0].shape
    kv_cut = cut - q_cut
    parcel = q_cut + DEPTHS * kv_cut

    def kernel(place_ref, *refs):
        ins, weight_ref = refs[:8], refs[8]
        hidden_ref, gains_ref = refs[9], refs[10]
        outs = refs[11:]
        depth = place_ref[1]
        pick = lax.broadcasted_iota(jnp.int32, (8, 128), 1) == (
            lax.broadcasted_iota(jnp.int32, (8, 128), 0) + (cut - 128)
        )
        gains = dot_nt(pick.astype(F32).astype(BF), weight_ref[:, 128:256])
        gains_ref[...] = gains
        gain = gains[0:1]
        for index in range(8):
            side, step = index // DEPTHS, index % DEPTHS
            value = ins[index][...].astype(F32)
            factor = lax.rsqrt(jnp.mean(value * value, axis=-1, keepdims=True) + EPS)
            hidden = (value * factor * gain).astype(BF)
            hidden_ref[index] = hidden
            block = jnp.transpose(dot(hidden, weight_ref[:, :256])).astype(BF)
            outs[step][side, :q_cut] = block[:q_cut]
            at = (depth + STEPS[step]) % DEPTHS
            at = pl.multiple_of(q_cut + kv_cut * at, 16)
            for out in outs:
                out[side, pl.ds(at, kv_cut)] = block[q_cut:cut]

    return run(
        2.2, kernel,
        [((8, rows, width), BF), ((8, width), F32)] + [((2, parcel, rows), BF)] * DEPTHS,
        list(inputs) + [weight],
        place,
    )


def attend(place, mine, theirs, cosine, sine, q_cut, k_cut):
    parcel, rows = mine[0].shape[1:]
    heads = RANKS * q_cut // HEAD
    heads_kv = RANKS * k_cut // HEAD
    keys = DEPTHS * rows
    group = heads // heads_kv
    per_side = heads // 2

    def kernel(place_ref, *refs):
        ins = refs[:8]
        cosine_ref, sine_ref = refs[8], refs[9]
        query_ref, key_ref, value_ref, stat_ref, mixed_ref = refs[10:15]
        core, depth = place_ref[0], place_ref[1]
        for index in range(8):
            side, step = index // DEPTHS, index % DEPTHS
            rank = side * DEPTHS + (depth + STEPS[step]) % DEPTHS
            block = ins[index]
            query_ref[pl.ds(pl.multiple_of(rank * q_cut, 16), q_cut)] = block[0, :q_cut]
            at = pl.ds(pl.multiple_of(rank * k_cut, 16), k_cut)
            for part in range(DEPTHS):
                low = q_cut + 2 * k_cut * part
                lanes = slice(part * rows, (part + 1) * rows)
                key_ref[at, lanes] = block[0, low : low + k_cut]
                value_ref[at, lanes] = block[0, low + k_cut : low + 2 * k_cut]
        here = pl.ds(pl.multiple_of(depth * rows, rows), rows)
        own_cosine, own_sine = cosine_ref[:, here], sine_ref[:, here]
        for head in range(heads):
            at = slice(head * HEAD, (head + 1) * HEAD)
            query_ref[at] = turned(query_ref[at].astype(F32), own_cosine, own_sine).astype(BF)
        all_cosine, all_sine = cosine_ref[...], sine_ref[...]
        for head in range(heads_kv):
            at = slice(head * HEAD, (head + 1) * HEAD)
            key_ref[at] = turned(key_ref[at].astype(F32), all_cosine, all_sine).astype(BF)
        allowed = mask_of(place_ref, rows, keys)
        lane = lax.broadcasted_iota(jnp.int32, (rows, 128), 1)
        stats = jnp.zeros((rows, 128), F32)
        for head in range(heads):
            kv = slice(head // group * HEAD, (head // group + 1) * HEAD)
            query = query_ref[head * HEAD : (head + 1) * HEAD]
            scores = dot_tn(query, key_ref[kv]) * HEAD ** (-0.5)
            scores = jnp.where(allowed, scores, -1e30)
            peak = jnp.max(scores, axis=-1, keepdims=True)
            weights = jnp.exp(scores - peak)
            total = jnp.sum(weights, axis=-1, keepdims=True)
            weights = (weights * (1.0 / total)).astype(BF)
            stats = jnp.where(lane == head, peak + jnp.log(total), stats)
            mixed = dot_nt(value_ref[kv], weights).astype(BF)
            side = head // per_side
            where = core if side == 0 else 1 - core
            at = where * (per_side * HEAD) + head % per_side * HEAD
            mixed_ref[pl.ds(pl.multiple_of(at, 16), HEAD)] = mixed
        stat_ref[...] = stats

    return run(
        5.0, kernel,
        [
            ((heads * HEAD, rows), BF),
            ((heads_kv * HEAD, keys), BF),
            ((heads_kv * HEAD, keys), BF),
            ((rows, 128), F32),
            ((heads * HEAD, rows), BF),
        ],
        list(mine) + list(theirs) + [cosine, sine],
        place,
        vmem=58,
        fetch=True,
        read=halves(4, 0, (parcel, rows))
        + halves(4, 1, (parcel, rows))
        + [pl.BlockSpec(cosine.shape, lambda i: (0, 0))] * 2,
    )


def mask_of(place_ref, rows, keys):
    here = place_ref[1] * rows
    row = lax.broadcasted_iota(jnp.int32, (rows, 1), 0) + here
    key = lax.broadcasted_iota(jnp.int32, (1, keys), 1)
    row_start, key_start = jnp.zeros_like(row), jnp.zeros_like(key)
    for index in range(2, 6):
        start = place_ref[index]
        row_start = jnp.maximum(row_start, jnp.where(row >= start, start, 0))
        key_start = jnp.maximum(key_start, jnp.where(key >= start, start, 0))
    return (row_start == key_start) & (key <= row)


def attend_back(place, query, key, value, stats, grad_mixed, cosine, sine, q_cut, k_cut):
    rows, keys = query.shape[1], key.shape[1]
    heads, heads_kv = query.shape[0] // HEAD, key.shape[0] // HEAD
    group = heads // heads_kv
    per_side = heads // 2
    scale = HEAD ** (-0.5)
    parcel = q_cut + 2 * DEPTHS * k_cut

    def kernel(place_ref, q_ref, k_ref, v_ref, stat_ref, grad_ref, cosine_ref, sine_ref, *refs):
        outs, (dq_ref, dk_ref, dv_ref) = refs[:DEPTHS], refs[DEPTHS:]
        core, depth = place_ref[0], place_ref[1]
        here = pl.ds(pl.multiple_of(depth * rows, rows), rows)
        own_cosine, own_sine = cosine_ref[:, here], -sine_ref[:, here]
        all_cosine, all_sine = cosine_ref[...], -sine_ref[...]
        allowed = mask_of(place_ref, rows, keys)
        for kv_head in range(heads_kv):
            kv = slice(kv_head * HEAD, (kv_head + 1) * HEAD)
            grad_key = jnp.zeros((HEAD, keys), F32)
            grad_value = jnp.zeros((HEAD, keys), F32)
            for head in range(kv_head * group, (kv_head + 1) * group):
                at = slice(head * HEAD, (head + 1) * HEAD)
                where = core if head < per_side else 1 - core
                low = where * (per_side * HEAD) + head % per_side * HEAD
                grad = grad_ref[pl.ds(pl.multiple_of(low, 16), HEAD)]
                scores = dot_tn(q_ref[at], k_ref[kv]) * scale
                scores = jnp.where(allowed, scores, -1e30)
                weights = jnp.exp(scores - stat_ref[:, head : head + 1])
                grad_weights = dot_tn(grad, v_ref[kv])
                centre = jnp.sum(weights * grad_weights, axis=-1, keepdims=True)
                grad_scores = (weights * (grad_weights - centre)).astype(BF)
                grad_query = dot_nt(k_ref[kv], grad_scores) * scale
                dq_ref[at] = turned(grad_query, own_cosine, own_sine).astype(BF)
                grad_key += dot(q_ref[at], grad_scores)
                grad_value += dot(grad, weights.astype(BF))
            dk_ref[kv] = turned(grad_key * scale, all_cosine, all_sine).astype(BF)
            dv_ref[kv] = grad_value.astype(BF)
        for index in range(8):
            side, step = index // DEPTHS, index % DEPTHS
            rank = side * DEPTHS + (depth + STEPS[step]) % DEPTHS
            out = outs[step]
            out[side, :q_cut] = dq_ref[pl.ds(pl.multiple_of(rank * q_cut, 16), q_cut)]
            at = pl.ds(pl.multiple_of(rank * k_cut, 16), k_cut)
            for part in range(DEPTHS):
                low = q_cut + 2 * k_cut * part
                lanes = slice(part * rows, (part + 1) * rows)
                out[side, low : low + k_cut] = dk_ref[at, lanes]
                out[side, low + k_cut : low + 2 * k_cut] = dv_ref[at, lanes]

    return run(
        20.0, kernel,
        [((2, parcel, rows), BF)] * DEPTHS,
        [query, key, value, stats, grad_mixed, cosine, sine],
        place,
        scratch=[
            pltpu.VMEM(query.shape, BF),
            pltpu.VMEM(key.shape, BF),
            pltpu.VMEM(key.shape, BF),
        ],
    )


def project_back(place, mine, theirs, hidden, parcel_in, q_cut, k_cut):
    parcel, rows = mine[0].shape[1:]
    width = hidden.shape[2]
    kv_cut = 2 * k_cut
    cut = q_cut + kv_cut
    block_rows = width // PLANES

    def kernel(place_ref, *refs):
        ins = refs[:8]
        hidden_home, parcel_ref, rows_ref, out_ref, hidden_ref, done = refs[8:]
        fetch = pltpu.make_async_copy(hidden_home, hidden_ref, done)
        fetch.start()
        out_ref[:, :, 256:] = parcel_ref[...]
        depth = place_ref[1]
        for index in range(8):
            side, step = index // DEPTHS, index % DEPTHS
            at = pl.multiple_of(q_cut + kv_cut * ((depth + STEPS[step]) % DEPTHS), 16)
            kv = sum(
                ins[side * DEPTHS + other][0, pl.ds(at, kv_cut)].astype(F32)
                for other in range(DEPTHS)
            )
            block = jnp.concatenate(
                [ins[index][0, :q_cut].astype(F32), kv, jnp.zeros((256 - cut, rows), F32)], axis=0
            )
            rows_ref[index] = jnp.transpose(block).astype(BF)
        fetch.wait()
        grad = dot_tn(hidden_ref[...].reshape(-1, width), rows_ref[...].reshape(-1, 256))
        out_ref[:, :, :256] = grad.astype(BF).reshape(PLANES, block_rows, 256)

    return run(
        1.8, kernel,
        [((8, rows, 256), BF), ((PLANES, block_rows, 256 + parcel_in.shape[2]), BF)],
        list(mine) + list(theirs) + [hidden, parcel_in],
        place,
        read=halves(4, 0, (parcel, rows))
        + halves(4, 1, (parcel, rows))
        + [AWAY, WHOLE],
        scratch=[pltpu.VMEM(hidden.shape, BF), pltpu.SemaphoreType.DMA],
    )


def side_product(left, right):
    rows, width = left.shape[1], right.shape[0]

    def kernel(left_ref, right_ref, own_ref, other_ref):
        own = dot_nt(left_ref[:DEPTHS].reshape(DEPTHS * rows, -1), right_ref[:, :256])
        own_ref[...] = own.reshape(DEPTHS, rows, width)
        other = dot_nt(left_ref[DEPTHS:].reshape(DEPTHS * rows, -1), right_ref[:, :256])
        other_ref[...] = other.astype(BF).reshape(DEPTHS, rows, width)

    return run(
        1.0, kernel,
        [((DEPTHS, rows, width), F32), ((DEPTHS, rows, width), BF)],
        [left, right],
    )


def side_outputs(own, other, weight):
    rows, width = own.shape[0] // DEPTHS, weight.shape[1]

    def kernel(own_in, other_in, weight_ref, own_ref, other_ref):
        own_ref[...] = dot(own_in[...], weight_ref[...]).reshape(DEPTHS, rows, width)
        other_ref[...] = dot(other_in[...], weight_ref[...]).astype(BF).reshape(DEPTHS, rows, width)

    return run(
        1.5, kernel,
        [((DEPTHS, rows, width), F32), ((DEPTHS, rows, width), BF)],
        [own, other, weight],
    )


def feed_forward(hidden, upstream, weight, down, kind):
    rows, width = hidden[0].shape
    inner_width = down.shape[0]

    def kernel(*refs):
        ins, ups = refs[:DEPTHS], refs[DEPTHS : 2 * DEPTHS]
        weight_ref, down_ref, inner_ref, grad_ref, out_ref = refs[2 * DEPTHS : 2 * DEPTHS + 5]
        rows_ref, expanded_ref, back_ref = refs[2 * DEPTHS + 5 :]
        for block in range(DEPTHS):
            at = slice(block * rows, (block + 1) * rows)
            rows_ref[at] = ins[block][...]
        expanded_ref[...] = dot(rows_ref[...], weight_ref[:, : 2 * inner_width])
        for block in range(DEPTHS):
            at = slice(block * rows, (block + 1) * rows)
            rows_ref[at] = ups[block][...]
        back_ref[...] = dot_nt(rows_ref[...], down_ref[...])
        for block in range(DEPTHS):
            at = slice(block * rows, (block + 1) * rows)
            gate, up_values = expanded_ref[at, :inner_width], expanded_ref[at, inner_width:]
            gate_sigmoid = jax.nn.sigmoid(gate)
            activated = gate * gate_sigmoid
            inner_ref[at] = (activated * up_values).astype(BF)
            grad_inner = back_ref[at]
            grad_ref[at, inner_width:] = (grad_inner * activated).astype(BF)
            grad_ref[at, :inner_width] = (
                grad_inner * up_values * gate_sigmoid * (1.0 + gate * (1.0 - gate_sigmoid))
            ).astype(BF)
        partial = dot_nt(grad_ref[...], weight_ref[:, : 2 * inner_width])
        out_ref[...] = partial.astype(kind).reshape(DEPTHS, rows, width)

    return run(
        5.6, kernel,
        [
            ((DEPTHS * rows, inner_width), BF),
            ((DEPTHS * rows, 2 * inner_width), BF),
            ((DEPTHS, rows, width), kind),
        ],
        list(hidden) + list(upstream) + [weight, down],
        scratch=[
            pltpu.VMEM((DEPTHS * rows, width), BF),
            pltpu.VMEM((DEPTHS * rows, 2 * inner_width), F32),
            pltpu.VMEM((DEPTHS * rows, inner_width), F32),
        ],
    )


def add_sides(own, received):
    rows, width = own.shape[1:]

    def kernel(own_ref, received_ref, *outs):
        for step in range(DEPTHS):
            total = own_ref[step] + received_ref[step].astype(F32)
            outs[step][...] = total.astype(outs[step].dtype)

    return run(
        1.0, kernel,
        [((rows, width), F32)] + [((rows, width), BF)] * (DEPTHS - 1),
        [own, received],
    )


def ffn_gradients(hidden, grads, inner, upstream):
    rows, width = hidden[0].shape
    expanded = grads[0].shape[1]
    inner_width = inner[0].shape[1]
    third = width // 3
    block_rows, rank_rows = width // PLANES, inner_width // PLANES

    def kernel(*refs):
        hid, ups = refs[:8], refs[8:16]
        grad_own, grad_other, inner_own, inner_other, out_ref, hidden_all, upstream_all = refs[16:]
        for index in range(8):
            at = slice(index * rows, (index + 1) * rows)
            hidden_all[at] = hid[index][...]
            upstream_all[at] = ups[index][...]
        split = DEPTHS * rows
        total = dot_tn(hidden_all[:split], grad_own[...]) + dot_tn(hidden_all[split:], grad_other[...])
        out_ref[:, :, :expanded] = total.astype(BF).reshape(PLANES, block_rows, expanded)
        total = dot_tn(inner_own[...], upstream_all[:split]) + dot_tn(
            inner_other[...], upstream_all[split:]
        )
        total = total.astype(BF).reshape(PLANES, rank_rows, width)
        for part in range(3):
            out_ref[:, part * rank_rows : (part + 1) * rank_rows, expanded:] = total[
                :, :, part * third : (part + 1) * third
            ]

    return run(
        5.0, kernel,
        [((PLANES, block_rows, expanded + third), BF)],
        list(hidden) + list(upstream) + list(grads) + list(inner),
        scratch=[pltpu.VMEM((8 * rows, width), BF)] * 2,
    )[0]


def into_residual(place, mixed, tokens, own_half, other_half, gains):
    half = tokens.shape[1] // 2

    def kernel(place_ref, mixed_ref, tokens_ref, own_ref, other_ref, gains_ref, residual_ref, hidden_ref):
        first = place_ref[0] == 0
        own = dot_tn(mixed_ref[...], own_ref[...])[:, :half]
        other = dot_tn(mixed_ref[...], other_ref[...])[:, :half]
        added = jnp.concatenate(
            [jnp.where(first, own, other), jnp.where(first, other, own)], axis=1
        )
        residual = tokens_ref[...].astype(F32) + added
        residual_ref[...] = residual
        factor = lax.rsqrt(jnp.mean(residual * residual, axis=-1, keepdims=True) + EPS)
        hidden_ref[...] = (residual * factor * gains_ref[1:2]).astype(BF)

    return run(
        1.5, kernel,
        [(tokens.shape, F32), (tokens.shape, BF)],
        [mixed, tokens, own_half, other_half, gains],
        place,
    )


def residual_back(place, parts, residual, upstream, own_half, other_half, gains):
    rows, width = residual.shape
    half, padded = width // 2, own_half.shape[1]

    def kernel(place_ref, *refs):
        ins = refs[:DEPTHS]
        residual_ref, upstream_ref, own_ref, other_ref, gains_ref = refs[DEPTHS : DEPTHS + 5]
        grad_ref, low_ref, mixed_ref = refs[DEPTHS + 5 :]
        grad = sum(part[...].astype(F32) for part in ins) * gains_ref[1:2]
        value = residual_ref[...]
        factor = lax.rsqrt(jnp.mean(value * value, axis=-1, keepdims=True) + EPS)
        grad = upstream_ref[...].astype(F32) + norm_back(grad, value * factor, factor)
        grad_ref[...] = grad
        low_ref[...] = grad.astype(BF)
        first = place_ref[0] == 0
        left, right = grad[:, :half], grad[:, half:]
        spare = jnp.zeros((rows, padded - half), F32)
        own = jnp.concatenate([jnp.where(first, left, right), spare], axis=1).astype(BF)
        other = jnp.concatenate([jnp.where(first, right, left), spare], axis=1).astype(BF)
        mixed = dot_nt(own_ref[...], own) + dot_nt(other_ref[...], other)
        mixed_ref[...] = mixed.astype(BF)

    return run(
        2.4, kernel,
        [(residual.shape, F32), (residual.shape, BF), ((own_half.shape[0], rows), BF)],
        list(parts) + [residual, upstream, own_half, other_half, gains],
        place,
    )


def inputs_back(parts, tokens, grad_residual, gains):
    def kernel(*refs):
        ins = refs[:DEPTHS]
        tokens_ref, residual_ref, gains_ref, out_ref = refs[DEPTHS:]
        grad = sum(part[...].astype(F32) for part in ins) * gains_ref[0:1]
        value = tokens_ref[...].astype(F32)
        factor = lax.rsqrt(jnp.mean(value * value, axis=-1, keepdims=True) + EPS)
        out_ref[...] = residual_ref[...] + norm_back(grad, value * factor, factor)

    return run(
        1.2, kernel, [(grad_residual.shape, F32)], list(parts) + [tokens, grad_residual, gains]
    )[0]


def output_gradient(place, mixed, mixed_other, low, low_other, padded):
    rows, width = low.shape
    half = width // 2

    def kernel(place_ref, mixed_ref, mixed_other_ref, low_ref, low_other_ref, out_ref):
        first = place_ref[0] == 0
        spare = jnp.zeros((rows, padded - half), F32)
        total = 0.0
        for heads_ref, grad_ref in ((mixed_ref, low_ref), (mixed_other_ref, low_other_ref)):
            grad = grad_ref[...].astype(F32)
            grad = jnp.where(first, grad[:, :half], grad[:, half:])
            grad = jnp.concatenate([grad, spare], axis=1).astype(BF)
            total = total + dot(heads_ref[...], grad)
        out_ref[...] = total.astype(BF).reshape(PLANES, -1, padded)

    return run(
        1.6, kernel,
        [((PLANES, mixed.shape[0] // PLANES, padded), BF)],
        [mixed, mixed_other, low, low_other],
        place,
    )[0]


BLOCKS = 13


def as_column(row, count):
    one = lax.broadcasted_iota(jnp.int32, (count, count), 0)
    other = lax.broadcasted_iota(jnp.int32, (count, count), 1)
    return jnp.sum(jnp.where(one == other, row, 0.0), axis=1, keepdims=True)


def packed(blocks):
    rows = sum(block.shape[0] for block in blocks)
    spare = jnp.zeros((-rows % 8, 128), F32)
    return jnp.concatenate(list(blocks) + [spare], axis=0).astype(BF)


def prepare(segments, source, first_gain, second_gain, query, key, value, output, gate, up):
    own, width = query.shape
    q_cut, k_cut = width // RANKS, key.shape[1] // RANKS
    rank_cut = gate.shape[1] // RANKS
    piece = rank_cut // PLANES
    half = width // 2

    values = [segments, source, first_gain, second_gain, query, key, value, output, gate, up]

    def kernel(seg_ref, src_ref, one_ref, two_ref, q_ref, k_ref, v_ref, o_ref, g_ref, u_ref, out_ref):
        lane = lax.broadcasted_iota(jnp.int32, (own, 16), 1)
        tail = jnp.where(
            lane == 0,
            as_column(one_ref[...].astype(F32), own),
            jnp.where(lane == 1, as_column(two_ref[...].astype(F32), own), 0.0),
        )
        slot = lax.broadcasted_iota(jnp.int32, (1, seg_ref.shape[1]), 1)
        for buffer in range(2):
            src = src_ref[buffer : buffer + 1]
            full = (seg_ref[buffer : buffer + 1] != -1).astype(jnp.int32)
            filled = jnp.sum(full, axis=1, keepdims=True)
            at_first = jnp.sum(jnp.where(slot == 0, src, 0), axis=1, keepdims=True)
            at_pad = jnp.sum(jnp.where(slot == filled, src, 0), axis=1, keepdims=True)
            marks = (filled, at_first >> 1, at_first & 1, at_pad >> 1, at_pad & 1)
            for index, mark in enumerate(marks):
                tail = jnp.where(lane == 2 + 2 * index + buffer, mark.astype(F32), tail)
        q, k, v = q_ref[...].astype(F32), k_ref[...].astype(F32), v_ref[...].astype(F32)
        o, g, u = o_ref[...].astype(F32), g_ref[...].astype(F32), u_ref[...].astype(F32)
        sides = []
        for side in range(2):
            padded = jnp.concatenate(
                [o[:, side * half : (side + 1) * half], jnp.zeros((own, 64), F32)], axis=1
            )
            sides.append([padded[:, 128 * i : 128 * (i + 1)] for i in range(5)])
        for rank in range(RANKS):
            blocks = [
                q[:, q_cut * rank : q_cut * rank + 128],
                jnp.concatenate(
                    [
                        q[:, q_cut * rank + 128 : q_cut * (rank + 1)],
                        k[:, k_cut * rank : k_cut * (rank + 1)],
                        v[:, k_cut * rank : k_cut * (rank + 1)],
                        tail,
                    ],
                    axis=1,
                ),
            ]
            for weight in (g, u):
                cut = jnp.concatenate(
                    [
                        weight[:, low : low + piece]
                        for low in range(piece * rank, RANKS * rank_cut, RANKS * piece)
                    ],
                    axis=1,
                )
                blocks += [cut[:, 128 * i : 128 * (i + 1)] for i in range(rank_cut // 128)]
            out_ref[rank] = packed(blocks + sides[rank // DEPTHS])

    rows = own * BLOCKS
    return run(
        3.2, kernel,
        [((RANKS, rows + -rows % 8, 128), BF)],
        values,
        vmem=60,
        fetch=True,
    )[0]


def assemble(column, own, blocks, down=None):
    wide = 128 * len(blocks)
    third = 0 if down is None else down.shape[1] // 3
    rows = RANKS * own

    def kernel(column_ref, *refs):
        out_ref = refs[-1]
        parts = []
        for block in blocks:
            parts.append(
                jnp.concatenate(
                    [
                        column_ref[rank, block * own : (block + 1) * own].astype(F32)
                        for rank in range(RANKS)
                    ],
                    axis=0,
                ).astype(BF)
            )
        if down is not None:
            parts.append(
                jnp.concatenate(
                    [refs[0][:, third * i : third * (i + 1)] for i in range(3)], axis=0
                )
            )
        whole = jnp.concatenate(parts, axis=1)
        for plane in range(PLANES):
            out_ref[plane] = whole

    return run(
        1.2, kernel,
        [((PLANES, rows, wide + third), BF)],
        [column] if down is None else [column, down],
    )[0]


def unpack_down(gathered, rank_rows, wide):
    planes, rows, columns = gathered.shape
    third = columns - wide

    def kernel(in_ref, out_ref):
        for plane in range(planes):
            for part in range(3):
                out_ref[
                    plane * rank_rows : (plane + 1) * rank_rows, third * part : third * (part + 1)
                ] = in_ref[plane, part * rank_rows : (part + 1) * rank_rows, wide:]

    return run(1.9, kernel, [((planes * rank_rows, 3 * third), BF)], [gathered])[0]


def sum_ffn(received, rank_rows, wide):
    planes, rows, columns = received.shape
    third = columns - wide

    def kernel(in_ref, sum_ref, down_ref):
        total = in_ref[0].astype(F32)
        for plane in range(1, planes):
            total = total + in_ref[plane].astype(F32)
        sum_ref[...] = total[:, :wide]
        for part in range(3):
            down_ref[:, third * part : third * (part + 1)] = total[
                part * rank_rows : (part + 1) * rank_rows, wide:
            ]

    return run(0.8, kernel, [((rows, wide), F32), ((rank_rows, 3 * third), F32)], [received])


def send_sums(attention, ffn, own):
    def kernel(attention_ref, ffn_ref, out_ref):
        total = attention_ref[0].astype(F32)
        for plane in range(1, PLANES):
            total = total + attention_ref[plane].astype(F32)
        wholes = [total[:, :256], ffn_ref[...], total[:, 256:]]
        for rank in range(RANKS):
            at = slice(rank * own, (rank + 1) * own)
            out_ref[rank] = packed(
                [
                    whole[at, 128 * i : 128 * (i + 1)]
                    for whole in wholes
                    for i in range(whole.shape[1] // 128)
                ]
            )

    rows = own * BLOCKS
    return run(
        2.7, kernel, [((RANKS, rows + -rows % 8, 128), BF)], [attention, ffn]
    )[0]


def finish(received, first_gain, second_gain, query, key, value, gate, up):
    own, width = query.shape
    q_cut, k_cut = width // RANKS, key.shape[1] // RANKS
    rank_cut = gate.shape[1] // RANKS
    piece = rank_cut // PLANES
    half = width // 2

    def kernel(in_ref, one_ref, two_ref, q_in, k_in, v_in, g_in, u_in, *outs):
        one_out, q_out, k_out, v_out, o_out, two_out, g_out, u_out = outs

        def block(rank, index):
            return in_ref[rank, index * own : (index + 1) * own].astype(F32)

        second = [block(rank, 1) for rank in range(RANKS)]
        q_parts = []
        for rank in range(RANKS):
            q_parts += [block(rank, 0), second[rank][:, : q_cut - 128]]
        low = q_cut - 128
        q = jnp.concatenate(q_parts, axis=1)
        k = jnp.concatenate([part[:, low : low + k_cut] for part in second], axis=1)
        v = jnp.concatenate([part[:, low + k_cut : low + 2 * k_cut] for part in second], axis=1)
        q_out[...], k_out[...], v_out[...] = q, k, v
        ffn = []
        for base in (2, 2 + rank_cut // 128):
            wide = [
                jnp.concatenate([block(rank, base + i) for i in range(rank_cut // 128)], axis=1)
                for rank in range(RANKS)
            ]
            ffn.append(
                jnp.concatenate(
                    [
                        wide[rank][:, piece * plane : piece * (plane + 1)]
                        for plane in range(PLANES)
                        for rank in range(RANKS)
                    ],
                    axis=1,
                )
            )
        g_out[...], u_out[...] = ffn
        base = 2 + 2 * rank_cut // 128
        sides = []
        for side in range(2):
            parts = []
            for i in range(base, BLOCKS):
                total = block(side * DEPTHS, i)
                for step in range(1, DEPTHS):
                    total = total + block(side * DEPTHS + step, i)
                parts.append(total)
            sides.append(jnp.concatenate(parts, axis=1)[:, :half])
        o_out[...] = jnp.concatenate(sides, axis=1)

        def along(pairs):
            return sum(
                jnp.sum(grad * ref[...].astype(F32), axis=1, keepdims=True) for grad, ref in pairs
            )

        def as_row(column):
            rows = lax.broadcasted_iota(jnp.int32, (own, own), 0)
            columns = lax.broadcasted_iota(jnp.int32, (own, own), 1)
            return jnp.sum(jnp.where(rows == columns, column, 0.0), axis=0, keepdims=True)

        one_out[...] = as_row(along([(q, q_in), (k, k_in), (v, v_in)])) / one_ref[...].astype(F32)
        two_out[...] = as_row(along([(ffn[0], g_in), (ffn[1], u_in)])) / two_ref[...].astype(F32)

    return run(
        1.3, kernel,
        [
            ((1, own), F32),
            (query.shape, F32),
            (key.shape, F32),
            (value.shape, F32),
            (query.shape, F32),
            ((1, own), F32),
            (gate.shape, F32),
            (up.shape, F32),
        ],
        [received, first_gain, second_gain, query, key, value, gate, up],
    )


def norm_back(grad, normed, scale):
    return scale * (grad - normed * jnp.mean(grad * normed, axis=-1, keepdims=True))


def on_device(
    tokens,
    cotangent,
    segments,
    slot_source,
    first_gain,
    query_weight,
    key_projection,
    value_projection,
    output_weight,
    second_gain,
    gate_weight,
    up_weight,
    down_weight,
):
    core, depth = lax.axis_index("c"), lax.axis_index("z")
    rows, width = tokens.shape
    own = query_weight.shape[0]
    q_cut, k_cut = query_weight.shape[1] // RANKS, key_projection.shape[1] // RANKS
    rank_rows = down_weight.shape[0]
    wide = 2 * gate_weight.shape[1] // RANKS
    cut = q_cut + 2 * k_cut
    gain_one, gain_two = first_gain.reshape(1, own), second_gain.reshape(1, own)

    def column_blocks(value):
        mine = gather_depths(value)
        return mine, [exchange(block) for block in mine]

    def parcels_between(parcels):
        mine = scatter_depths(parcels)
        return mine, [exchange(block) for block in mine]

    inputs_mine, inputs_theirs = column_blocks(tokens)
    column = deal(
        prepare(
            segments[0],
            slot_source[0],
            gain_one,
            gain_two,
            query_weight,
            key_projection,
            value_projection,
            output_weight,
            gate_weight,
            up_weight,
        ),
        COLUMN,
    )
    attention_w = deal(assemble(column, own, range(2)), PLANE).reshape(width, -1)
    output_in = assemble(column, own, range(8, BLOCKS))
    ffn_in = assemble(column, own, range(2, 8), down_weight)

    marks = column.reshape(2, DEPTHS, -1, 128)[:, :, own, cut + 2 - 128 : cut + 12 - 128]
    marks = marks.astype(jnp.int32)
    marks = jnp.where(core == 0, marks[0], marks[1]).reshape(DEPTHS, 5, 2)
    padded = marks[:, 0] < segments.shape[2]
    earlier_padded = jnp.concatenate([jnp.zeros((1, 2), bool), padded[:-1]])
    pad_starts = jnp.sum(
        jnp.where(padded & ~earlier_padded, marks[:, 3] * 2 + marks[:, 4], 0), axis=0
    )
    starts = jnp.concatenate([marks[0, 1] * 2 + marks[0, 2], pad_starts])
    group_rows = jnp.arange(DEPTHS * rows)
    run_start = jnp.max(
        jnp.where(starts[None, :] <= group_rows[:, None], starts[None, :], 0), axis=1
    )
    frequency = THETA ** (-(jnp.arange(HEAD // 2).astype(F32) * 2.0 / HEAD))
    angles = frequency[:, None] * (group_rows - run_start).astype(F32)[None, :]
    cosine, sine = jnp.cos(angles), jnp.sin(angles)
    place = jnp.concatenate([jnp.stack([core, depth]), starts]).astype(jnp.int32)

    hidden_one, gains_full, *parcels = project(
        after(place, (cosine, sine)), inputs_mine + inputs_theirs, attention_w, cut, q_cut
    )
    output_own = deal(after(output_in, parcels[0]), PLANE)
    mine, theirs = parcels_between(parcels)
    upstream_mine = gather_depths(after(cotangent, theirs[3]))
    ffn_blocks = deal(after(ffn_in, (output_own, theirs)), PLANE)
    output_own = output_own.reshape(width, -1)
    output_other = exchange(output_own)
    down_w = unpack_down(ffn_blocks, rank_rows, wide)
    ffn_w = ffn_blocks.reshape(width, -1)
    query, key, value, stats, mixed = attend(place, mine, theirs, cosine, sine, q_cut, k_cut)

    residual, hidden_two = into_residual(
        place, mixed, tokens, output_own, output_other, gains_full
    )
    mixed_other = exchange(mixed)
    hidden_mine, hidden_theirs = column_blocks(after(hidden_two, mixed_other))
    upstream_theirs = [exchange(after(block, hidden_mine)) for block in upstream_mine]
    inner_theirs, grads_theirs, partial_theirs = feed_forward(
        hidden_theirs, upstream_theirs, ffn_w, down_w, BF
    )
    inner_mine, grads_mine, partial_mine = feed_forward(
        hidden_mine, upstream_mine, ffn_w, down_w, F32
    )
    ffn_grads = ffn_gradients(
        hidden_mine + hidden_theirs,
        [grads_mine, grads_theirs],
        [inner_mine, inner_theirs],
        upstream_mine + upstream_theirs,
    )
    parts = scatter_depths(add_sides(partial_mine, exchange(partial_theirs)))
    grad_residual, residual_low, grad_mixed = residual_back(
        after(place, ffn_grads), parts, residual, cotangent, output_own, output_other, gains_full
    )
    ffn_sum = deal(ffn_grads, PLANE)

    parcels = attend_back(
        place, query, key, value, stats, grad_mixed, cosine, sine, q_cut, k_cut
    )
    mine, theirs = parcels_between(parcels)
    output_grads = output_gradient(
        place,
        mixed,
        mixed_other,
        after(residual_low, parcels[0]),
        exchange(residual_low),
        output_own.shape[1],
    )
    projected_rows, attention_grads = project_back(
        place, mine, theirs, hidden_one, output_grads, q_cut, k_cut
    )
    attention_sum = deal(after(attention_grads, ffn_sum), PLANE)
    outputs_own, outputs_other = side_outputs(
        after(inner_mine, attention_grads), inner_theirs, down_w
    )
    outputs = add_sides(outputs_own, exchange(outputs_other))
    inputs_own, inputs_other = side_product(projected_rows, attention_w)
    parts = scatter_depths(add_sides(inputs_own, exchange(inputs_other)))
    gradient_tokens = inputs_back(parts, tokens, grad_residual, gains_full)
    outputs = [outputs[0]] + [after(part, parts[1:3]) for part in outputs[1:]]
    outputs = scatter_depths(outputs)
    layer_output = (residual + sum(part.astype(F32) for part in outputs)).astype(BF)

    ffn_sum, grad_down = sum_ffn(ffn_sum, rank_rows, wide)
    received = deal(send_sums(attention_sum, ffn_sum, own), COLUMN)
    one, grad_q, grad_k, grad_v, grad_o, two, grad_g, grad_u = finish(
        received,
        gain_one,
        gain_two,
        query_weight,
        key_projection,
        value_projection,
        gate_weight,
        up_weight,
    )
    return (
        layer_output,
        gradient_tokens,
        one.reshape(own),
        grad_q,
        grad_k,
        grad_v,
        grad_o,
        two.reshape(own),
        grad_g,
        grad_u,
        grad_down,
    )


def solution(mesh):
    grid = Mesh(mesh.devices.reshape(4, 4, 2, 4), ALL)
    rows = P(ALL, None)
    flat = P(ALL)
    slots = P(("y", "x", "c"), None, "z")
    return jax.shard_map(
        on_device,
        mesh=grid,
        in_specs=(rows, rows, slots, slots, flat, rows, rows, rows, rows, flat, rows, rows, rows),
        out_specs=(rows, rows, flat, rows, rows, rows, rows, flat, rows, rows, rows),
        check_vma=False,
    )
```

```python
import jax
import jax.numpy as jnp
from jax import lax
from jax.experimental import pallas as pl
from jax.experimental.pallas import tpu as pltpu
from jax.sharding import Mesh
from jax.sharding import PartitionSpec as P

HEAD = 64
EPS = 1e-05
THETA = 10000.0
BF = jnp.bfloat16
F32 = jnp.float32
ALL = ("y", "x", "c", "z")
COLUMN = ("c", "z")
PLANE = ("y", "x")
RANKS, PLANES, DEPTHS = 8, 16, 4
PARAMS = pltpu.CompilerParams(vmem_limit_bytes=56 * 1024 * 1024)


def dot(left, right):
    return jnp.dot(left, right, preferred_element_type=F32)


def dot_nt(left, right):
    return lax.dot_general(left, right, (((1,), (1,)), ((), ())), preferred_element_type=F32)


def dot_tn(left, right):
    return lax.dot_general(left, right, (((0,), (0,)), ((), ())), preferred_element_type=F32)


def exchange(value):
    return lax.ppermute(value, "c", [(0, 1), (1, 0)])


def deal(value, axes):
    return lax.all_to_all(value, axes, 0, 0, tiled=True)


def after(value, earlier):
    return lax.optimization_barrier((value, earlier))[0]


def from_depth(value, step):
    return lax.ppermute(value, "z", [(i, (i - step) % DEPTHS) for i in range(DEPTHS)])


def gather_depths(value):
    return [value, from_depth(value, 1), from_depth(value, 3), from_depth(value, 2)]


def scatter_depths(blocks):
    return [blocks[0], from_depth(blocks[2], 1), from_depth(blocks[1], 3), from_depth(blocks[3], 2)]


STEPS = (0, 1, 3, 2)


FLOPS_PER_MICRO = 1.15e9


def entire(shape):
    return pl.BlockSpec(shape, lambda i: (0,) * len(shape))


def run(
    micros, kernel, outs, values, scalars=None, scratch=(), vmem=16, read=None, fetch=False
):
    whole = pl.BlockSpec(memory_space=pltpu.VMEM)
    specs = [entire(value.shape) if fetch else whole for value in values] if read is None else list(read)
    if scalars is not None:
        values = [scalars] + list(values)
        specs = [pl.BlockSpec(memory_space=pltpu.SMEM)] + specs
    shapes = [jax.ShapeDtypeStruct(shape, dtype) for shape, dtype in outs]
    size = sum(v.size * v.dtype.itemsize for v in values)
    size += sum(o.size * o.dtype.itemsize for o in shapes)
    return pl.pallas_call(
        kernel,
        grid=(1,),
        in_specs=specs,
        out_specs=[entire(shape) if fetch else whole for shape, _ in outs],
        out_shape=shapes,
        scratch_shapes=list(scratch),
        compiler_params=pltpu.CompilerParams(vmem_limit_bytes=vmem * 1024 * 1024),
        cost_estimate=pl.CostEstimate(
            flops=int(micros * FLOPS_PER_MICRO), bytes_accessed=size, transcendentals=0
        ),
    )(*values)


WHOLE = pl.BlockSpec(memory_space=pltpu.VMEM)
AWAY = pl.BlockSpec(memory_space=pl.ANY)


def halves(count, which, shape):
    return [pl.BlockSpec((1,) + shape, lambda i: (which, 0, 0))] * count


def turned(value, cosine, sine):
    first, second = value[: HEAD // 2], value[HEAD // 2 :]
    return jnp.concatenate(
        [first * cosine - second * sine, first * sine + second * cosine], axis=0
    )


def project(place, inputs, weight, cut, q_cut):
    rows, width = inputs[0].shape
    kv_cut = cut - q_cut
    parcel = q_cut + DEPTHS * kv_cut

    def kernel(place_ref, *refs):
        ins, weight_ref = refs[:8], refs[8]
        hidden_ref, gains_ref = refs[9], refs[10]
        outs = refs[11:]
        depth = place_ref[1]
        pick = lax.broadcasted_iota(jnp.int32, (8, 128), 1) == (
            lax.broadcasted_iota(jnp.int32, (8, 128), 0) + (cut - 128)
        )
        gains = dot_nt(pick.astype(F32).astype(BF), weight_ref[:, 128:256])
        gains_ref[...] = gains
        gain = gains[0:1]
        for index in range(8):
            side, step = index // DEPTHS, index % DEPTHS
            value = ins[index][...].astype(F32)
            factor = lax.rsqrt(jnp.mean(value * value, axis=-1, keepdims=True) + EPS)
            hidden = (value * factor * gain).astype(BF)
            hidden_ref[index] = hidden
            block = jnp.transpose(dot(hidden, weight_ref[:, :256])).astype(BF)
            outs[step][side, :q_cut] = block[:q_cut]
            at = (depth + STEPS[step]) % DEPTHS
            at = pl.multiple_of(q_cut + kv_cut * at, 16)
            for out in outs:
                out[side, pl.ds(at, kv_cut)] = block[q_cut:cut]

    return run(
        2.2, kernel,
        [((8, rows, width), BF), ((8, width), F32)] + [((2, parcel, rows), BF)] * DEPTHS,
        list(inputs) + [weight],
        place,
    )


def attend(place, mine, theirs, cosine, sine, q_cut, k_cut):
    parcel, rows = mine[0].shape[1:]
    heads = RANKS * q_cut // HEAD
    heads_kv = RANKS * k_cut // HEAD
    keys = DEPTHS * rows
    group = heads // heads_kv
    per_side = heads // 2

    def kernel(place_ref, *refs):
        ins = refs[:8]
        cosine_ref, sine_ref = refs[8], refs[9]
        query_ref, key_ref, value_ref, stat_ref, mixed_ref = refs[10:15]
        core, depth = place_ref[0], place_ref[1]
        for index in range(8):
            side, step = index // DEPTHS, index % DEPTHS
            rank = side * DEPTHS + (depth + STEPS[step]) % DEPTHS
            block = ins[index]
            query_ref[pl.ds(pl.multiple_of(rank * q_cut, 16), q_cut)] = block[0, :q_cut]
            at = pl.ds(pl.multiple_of(rank * k_cut, 16), k_cut)
            for part in range(DEPTHS):
                low = q_cut + 2 * k_cut * part
                lanes = slice(part * rows, (part + 1) * rows)
                key_ref[at, lanes] = block[0, low : low + k_cut]
                value_ref[at, lanes] = block[0, low + k_cut : low + 2 * k_cut]
        here = pl.ds(pl.multiple_of(depth * rows, rows), rows)
        own_cosine, own_sine = cosine_ref[:, here], sine_ref[:, here]
        for head in range(heads):
            at = slice(head * HEAD, (head + 1) * HEAD)
            query_ref[at] = turned(query_ref[at].astype(F32), own_cosine, own_sine).astype(BF)
        all_cosine, all_sine = cosine_ref[...], sine_ref[...]
        for head in range(heads_kv):
            at = slice(head * HEAD, (head + 1) * HEAD)
            key_ref[at] = turned(key_ref[at].astype(F32), all_cosine, all_sine).astype(BF)
        allowed = mask_of(place_ref, rows, keys)
        lane = lax.broadcasted_iota(jnp.int32, (rows, 128), 1)
        stats = jnp.zeros((rows, 128), F32)
        for head in range(heads):
            kv = slice(head // group * HEAD, (head // group + 1) * HEAD)
            query = query_ref[head * HEAD : (head + 1) * HEAD]
            scores = dot_tn(query, key_ref[kv]) * HEAD ** (-0.5)
            scores = jnp.where(allowed, scores, -1e30)
            peak = jnp.max(scores, axis=-1, keepdims=True)
            weights = jnp.exp(scores - peak)
            total = jnp.sum(weights, axis=-1, keepdims=True)
            weights = (weights * (1.0 / total)).astype(BF)
            stats = jnp.where(lane == head, peak + jnp.log(total), stats)
            mixed = dot_nt(value_ref[kv], weights).astype(BF)
            side = head // per_side
            where = core if side == 0 else 1 - core
            at = where * (per_side * HEAD) + head % per_side * HEAD
            mixed_ref[pl.ds(pl.multiple_of(at, 16), HEAD)] = mixed
        stat_ref[...] = stats

    return run(
        5.0, kernel,
        [
            ((heads * HEAD, rows), BF),
            ((heads_kv * HEAD, keys), BF),
            ((heads_kv * HEAD, keys), BF),
            ((rows, 128), F32),
            ((heads * HEAD, rows), BF),
        ],
        list(mine) + list(theirs) + [cosine, sine],
        place,
        vmem=58,
        fetch=True,
        read=halves(4, 0, (parcel, rows))
        + halves(4, 1, (parcel, rows))
        + [pl.BlockSpec(cosine.shape, lambda i: (0, 0))] * 2,
    )


def mask_of(place_ref, rows, keys):
    here = place_ref[1] * rows
    row = lax.broadcasted_iota(jnp.int32, (rows, 1), 0) + here
    key = lax.broadcasted_iota(jnp.int32, (1, keys), 1)
    row_start, key_start = jnp.zeros_like(row), jnp.zeros_like(key)
    for index in range(2, 6):
        start = place_ref[index]
        row_start = jnp.maximum(row_start, jnp.where(row >= start, start, 0))
        key_start = jnp.maximum(key_start, jnp.where(key >= start, start, 0))
    return (row_start == key_start) & (key <= row)


def attend_back(place, query, key, value, stats, grad_mixed, cosine, sine, q_cut, k_cut):
    rows, keys = query.shape[1], key.shape[1]
    heads, heads_kv = query.shape[0] // HEAD, key.shape[0] // HEAD
    group = heads // heads_kv
    per_side = heads // 2
    scale = HEAD ** (-0.5)
    parcel = q_cut + 2 * DEPTHS * k_cut

    def kernel(place_ref, q_ref, k_ref, v_ref, stat_ref, grad_ref, cosine_ref, sine_ref, *refs):
        outs, (dq_ref, dk_ref, dv_ref) = refs[:DEPTHS], refs[DEPTHS:]
        core, depth = place_ref[0], place_ref[1]
        here = pl.ds(pl.multiple_of(depth * rows, rows), rows)
        own_cosine, own_sine = cosine_ref[:, here], -sine_ref[:, here]
        all_cosine, all_sine = cosine_ref[...], -sine_ref[...]
        allowed = mask_of(place_ref, rows, keys)
        for kv_head in range(heads_kv):
            kv = slice(kv_head * HEAD, (kv_head + 1) * HEAD)
            grad_key = jnp.zeros((HEAD, keys), F32)
            grad_value = jnp.zeros((HEAD, keys), F32)
            for head in range(kv_head * group, (kv_head + 1) * group):
                at = slice(head * HEAD, (head + 1) * HEAD)
                where = core if head < per_side else 1 - core
                low = where * (per_side * HEAD) + head % per_side * HEAD
                grad = grad_ref[pl.ds(pl.multiple_of(low, 16), HEAD)]
                scores = dot_tn(q_ref[at], k_ref[kv]) * scale
                scores = jnp.where(allowed, scores, -1e30)
                weights = jnp.exp(scores - stat_ref[:, head : head + 1])
                grad_weights = dot_tn(grad, v_ref[kv])
                centre = jnp.sum(weights * grad_weights, axis=-1, keepdims=True)
                grad_scores = (weights * (grad_weights - centre)).astype(BF)
                grad_query = dot_nt(k_ref[kv], grad_scores) * scale
                dq_ref[at] = turned(grad_query, own_cosine, own_sine).astype(BF)
                grad_key += dot(q_ref[at], grad_scores)
                grad_value += dot(grad, weights.astype(BF))
            dk_ref[kv] = turned(grad_key * scale, all_cosine, all_sine).astype(BF)
            dv_ref[kv] = grad_value.astype(BF)
        for index in range(8):
            side, step = index // DEPTHS, index % DEPTHS
            rank = side * DEPTHS + (depth + STEPS[step]) % DEPTHS
            out = outs[step]
            out[side, :q_cut] = dq_ref[pl.ds(pl.multiple_of(rank * q_cut, 16), q_cut)]
            at = pl.ds(pl.multiple_of(rank * k_cut, 16), k_cut)
            for part in range(DEPTHS):
                low = q_cut + 2 * k_cut * part
                lanes = slice(part * rows, (part + 1) * rows)
                out[side, low : low + k_cut] = dk_ref[at, lanes]
                out[side, low + k_cut : low + 2 * k_cut] = dv_ref[at, lanes]

    return run(
        20.0, kernel,
        [((2, parcel, rows), BF)] * DEPTHS,
        [query, key, value, stats, grad_mixed, cosine, sine],
        place,
        scratch=[
            pltpu.VMEM(query.shape, BF),
            pltpu.VMEM(key.shape, BF),
            pltpu.VMEM(key.shape, BF),
        ],
    )


def project_back(place, mine, theirs, hidden, parcel_in, q_cut, k_cut):
    parcel, rows = mine[0].shape[1:]
    width = hidden.shape[2]
    kv_cut = 2 * k_cut
    cut = q_cut + kv_cut
    block_rows = width // PLANES

    def kernel(place_ref, *refs):
        ins = refs[:8]
        hidden_home, parcel_ref, rows_ref, out_ref, hidden_ref, done = refs[8:]
        fetch = pltpu.make_async_copy(hidden_home, hidden_ref, done)
        fetch.start()
        out_ref[:, :, 256:] = parcel_ref[...]
        depth = place_ref[1]
        for index in range(8):
            side, step = index // DEPTHS, index % DEPTHS
            at = pl.multiple_of(q_cut + kv_cut * ((depth + STEPS[step]) % DEPTHS), 16)
            kv = sum(
                ins[side * DEPTHS + other][0, pl.ds(at, kv_cut)].astype(F32)
                for other in range(DEPTHS)
            )
            block = jnp.concatenate(
                [ins[index][0, :q_cut].astype(F32), kv, jnp.zeros((256 - cut, rows), F32)], axis=0
            )
            rows_ref[index] = jnp.transpose(block).astype(BF)
        fetch.wait()
        grad = dot_tn(hidden_ref[...].reshape(-1, width), rows_ref[...].reshape(-1, 256))
        out_ref[:, :, :256] = grad.astype(BF).reshape(PLANES, block_rows, 256)

    return run(
        1.8, kernel,
        [((8, rows, 256), BF), ((PLANES, block_rows, 256 + parcel_in.shape[2]), BF)],
        list(mine) + list(theirs) + [hidden, parcel_in],
        place,
        read=halves(4, 0, (parcel, rows))
        + halves(4, 1, (parcel, rows))
        + [AWAY, WHOLE],
        scratch=[pltpu.VMEM(hidden.shape, BF), pltpu.SemaphoreType.DMA],
    )


def side_product(left, right):
    rows, width = left.shape[1], right.shape[0]

    def kernel(left_ref, right_ref, own_ref, other_ref):
        own = dot_nt(left_ref[:DEPTHS].reshape(DEPTHS * rows, -1), right_ref[:, :256])
        own_ref[...] = own.reshape(DEPTHS, rows, width)
        other = dot_nt(left_ref[DEPTHS:].reshape(DEPTHS * rows, -1), right_ref[:, :256])
        other_ref[...] = other.astype(BF).reshape(DEPTHS, rows, width)

    return run(
        1.0, kernel,
        [((DEPTHS, rows, width), F32), ((DEPTHS, rows, width), BF)],
        [left, right],
    )


def side_outputs(own, other, weight):
    rows, width = own.shape[0] // DEPTHS, weight.shape[1]

    def kernel(own_in, other_in, weight_ref, own_ref, other_ref):
        own_ref[...] = dot(own_in[...], weight_ref[...]).reshape(DEPTHS, rows, width)
        other_ref[...] = dot(other_in[...], weight_ref[...]).astype(BF).reshape(DEPTHS, rows, width)

    return run(
        1.5, kernel,
        [((DEPTHS, rows, width), F32), ((DEPTHS, rows, width), BF)],
        [own, other, weight],
    )


def feed_forward(hidden, upstream, weight, down, kind):
    rows, width = hidden[0].shape
    inner_width = down.shape[0]

    def kernel(*refs):
        ins, ups = refs[:DEPTHS], refs[DEPTHS : 2 * DEPTHS]
        weight_ref, down_ref, inner_ref, grad_ref, out_ref = refs[2 * DEPTHS : 2 * DEPTHS + 5]
        rows_ref, expanded_ref, back_ref = refs[2 * DEPTHS + 5 :]
        for block in range(DEPTHS):
            at = slice(block * rows, (block + 1) * rows)
            rows_ref[at] = ins[block][...]
        expanded_ref[...] = dot(rows_ref[...], weight_ref[:, : 2 * inner_width])
        for block in range(DEPTHS):
            at = slice(block * rows, (block + 1) * rows)
            rows_ref[at] = ups[block][...]
        back_ref[...] = dot_nt(rows_ref[...], down_ref[...])
        for block in range(DEPTHS):
            at = slice(block * rows, (block + 1) * rows)
            gate, up_values = expanded_ref[at, :inner_width], expanded_ref[at, inner_width:]
            gate_sigmoid = jax.nn.sigmoid(gate)
            activated = gate * gate_sigmoid
            inner_ref[at] = (activated * up_values).astype(BF)
            grad_inner = back_ref[at]
            grad_ref[at, inner_width:] = (grad_inner * activated).astype(BF)
            grad_ref[at, :inner_width] = (
                grad_inner * up_values * gate_sigmoid * (1.0 + gate * (1.0 - gate_sigmoid))
            ).astype(BF)
        partial = dot_nt(grad_ref[...], weight_ref[:, : 2 * inner_width])
        out_ref[...] = partial.astype(kind).reshape(DEPTHS, rows, width)

    return run(
        5.6, kernel,
        [
            ((DEPTHS * rows, inner_width), BF),
            ((DEPTHS * rows, 2 * inner_width), BF),
            ((DEPTHS, rows, width), kind),
        ],
        list(hidden) + list(upstream) + [weight, down],
        scratch=[
            pltpu.VMEM((DEPTHS * rows, width), BF),
            pltpu.VMEM((DEPTHS * rows, 2 * inner_width), F32),
            pltpu.VMEM((DEPTHS * rows, inner_width), F32),
        ],
    )


def add_sides(own, received):
    rows, width = own.shape[1:]

    def kernel(own_ref, received_ref, *outs):
        for step in range(DEPTHS):
            total = own_ref[step] + received_ref[step].astype(F32)
            outs[step][...] = total.astype(outs[step].dtype)

    return run(
        1.0, kernel,
        [((rows, width), F32)] + [((rows, width), BF)] * (DEPTHS - 1),
        [own, received],
    )


def ffn_gradients(hidden, grads, inner, upstream):
    rows, width = hidden[0].shape
    expanded = grads[0].shape[1]
    inner_width = inner[0].shape[1]
    third = width // 3
    block_rows, rank_rows = width // PLANES, inner_width // PLANES

    def kernel(*refs):
        hid, ups = refs[:8], refs[8:16]
        grad_own, grad_other, inner_own, inner_other, out_ref = refs[16:21]
        hidden_all, upstream_all, grad_all, inner_all = refs[21:]
        for index in range(8):
            at = slice(index * rows, (index + 1) * rows)
            hidden_all[at] = hid[index][...]
            upstream_all[at] = ups[index][...]
        split = DEPTHS * rows
        grad_all[:split], grad_all[split:] = grad_own[...], grad_other[...]
        inner_all[:split], inner_all[split:] = inner_own[...], inner_other[...]
        total = dot_tn(hidden_all[...], grad_all[...])
        out_ref[:, :, :expanded] = total.astype(BF).reshape(PLANES, block_rows, expanded)
        total = dot_tn(inner_all[...], upstream_all[...])
        total = total.astype(BF).reshape(PLANES, rank_rows, width)
        for part in range(3):
            out_ref[:, part * rank_rows : (part + 1) * rank_rows, expanded:] = total[
                :, :, part * third : (part + 1) * third
            ]

    return run(
        5.0, kernel,
        [((PLANES, block_rows, expanded + third), BF)],
        list(hidden) + list(upstream) + list(grads) + list(inner),
        scratch=[pltpu.VMEM((8 * rows, width), BF)] * 2
        + [pltpu.VMEM((8 * rows, expanded), BF), pltpu.VMEM((8 * rows, inner_width), BF)],
    )[0]


def into_residual(place, mixed, tokens, own_half, other_half, gains):
    half = tokens.shape[1] // 2

    def kernel(place_ref, mixed_ref, tokens_ref, own_ref, other_ref, gains_ref, residual_ref, hidden_ref):
        first = place_ref[0] == 0
        own = dot_tn(mixed_ref[...], own_ref[...])[:, :half]
        other = dot_tn(mixed_ref[...], other_ref[...])[:, :half]
        added = jnp.concatenate(
            [jnp.where(first, own, other), jnp.where(first, other, own)], axis=1
        )
        residual = tokens_ref[...].astype(F32) + added
        residual_ref[...] = residual
        factor = lax.rsqrt(jnp.mean(residual * residual, axis=-1, keepdims=True) + EPS)
        hidden_ref[...] = (residual * factor * gains_ref[1:2]).astype(BF)

    return run(
        1.5, kernel,
        [(tokens.shape, F32), (tokens.shape, BF)],
        [mixed, tokens, own_half, other_half, gains],
        place,
    )


def residual_back(place, parts, residual, upstream, own_half, other_half, gains):
    rows, width = residual.shape
    half, padded = width // 2, own_half.shape[1]

    def kernel(place_ref, *refs):
        ins = refs[:DEPTHS]
        residual_ref, upstream_ref, own_ref, other_ref, gains_ref = refs[DEPTHS : DEPTHS + 5]
        grad_ref, low_ref, mixed_ref = refs[DEPTHS + 5 :]
        grad = sum(part[...].astype(F32) for part in ins) * gains_ref[1:2]
        value = residual_ref[...]
        factor = lax.rsqrt(jnp.mean(value * value, axis=-1, keepdims=True) + EPS)
        grad = upstream_ref[...].astype(F32) + norm_back(grad, value * factor, factor)
        grad_ref[...] = grad
        low_ref[...] = grad.astype(BF)
        first = place_ref[0] == 0
        left, right = grad[:, :half], grad[:, half:]
        spare = jnp.zeros((rows, padded - half), F32)
        own = jnp.concatenate([jnp.where(first, left, right), spare], axis=1).astype(BF)
        other = jnp.concatenate([jnp.where(first, right, left), spare], axis=1).astype(BF)
        mixed = dot_nt(own_ref[...], own) + dot_nt(other_ref[...], other)
        mixed_ref[...] = mixed.astype(BF)

    return run(
        2.4, kernel,
        [(residual.shape, F32), (residual.shape, BF), ((own_half.shape[0], rows), BF)],
        list(parts) + [residual, upstream, own_half, other_half, gains],
        place,
    )


def inputs_back(parts, tokens, grad_residual, gains):
    def kernel(*refs):
        ins = refs[:DEPTHS]
        tokens_ref, residual_ref, gains_ref, out_ref = refs[DEPTHS:]
        grad = sum(part[...].astype(F32) for part in ins) * gains_ref[0:1]
        value = tokens_ref[...].astype(F32)
        factor = lax.rsqrt(jnp.mean(value * value, axis=-1, keepdims=True) + EPS)
        out_ref[...] = residual_ref[...] + norm_back(grad, value * factor, factor)

    return run(
        1.2, kernel, [(grad_residual.shape, F32)], list(parts) + [tokens, grad_residual, gains]
    )[0]


def output_gradient(place, mixed, mixed_other, low, low_other, padded):
    rows, width = low.shape
    half = width // 2

    def kernel(place_ref, mixed_ref, mixed_other_ref, low_ref, low_other_ref, out_ref):
        first = place_ref[0] == 0
        spare = jnp.zeros((rows, padded - half), F32)
        total = 0.0
        for heads_ref, grad_ref in ((mixed_ref, low_ref), (mixed_other_ref, low_other_ref)):
            grad = grad_ref[...].astype(F32)
            grad = jnp.where(first, grad[:, :half], grad[:, half:])
            grad = jnp.concatenate([grad, spare], axis=1).astype(BF)
            total = total + dot(heads_ref[...], grad)
        out_ref[...] = total.astype(BF).reshape(PLANES, -1, padded)

    return run(
        1.6, kernel,
        [((PLANES, mixed.shape[0] // PLANES, padded), BF)],
        [mixed, mixed_other, low, low_other],
        place,
    )[0]


BLOCKS = 13


def as_column(row, count):
    one = lax.broadcasted_iota(jnp.int32, (count, count), 0)
    other = lax.broadcasted_iota(jnp.int32, (count, count), 1)
    return jnp.sum(jnp.where(one == other, row, 0.0), axis=1, keepdims=True)


def packed(blocks):
    rows = sum(block.shape[0] for block in blocks)
    spare = jnp.zeros((-rows % 8, 128), F32)
    return jnp.concatenate(list(blocks) + [spare], axis=0).astype(BF)


def prepare(segments, source, first_gain, second_gain, query, key, value, output, gate, up):
    own, width = query.shape
    q_cut, k_cut = width // RANKS, key.shape[1] // RANKS
    rank_cut = gate.shape[1] // RANKS
    piece = rank_cut // PLANES
    half = width // 2

    values = [segments, source, first_gain, second_gain, query, key, value, output, gate, up]

    def kernel(seg_ref, src_ref, one_ref, two_ref, q_ref, k_ref, v_ref, o_ref, g_ref, u_ref, out_ref):
        lane = lax.broadcasted_iota(jnp.int32, (own, 16), 1)
        tail = jnp.where(
            lane == 0,
            as_column(one_ref[...].astype(F32), own),
            jnp.where(lane == 1, as_column(two_ref[...].astype(F32), own), 0.0),
        )
        slot = lax.broadcasted_iota(jnp.int32, (1, seg_ref.shape[1]), 1)
        for buffer in range(2):
            src = src_ref[buffer : buffer + 1]
            full = (seg_ref[buffer : buffer + 1] != -1).astype(jnp.int32)
            filled = jnp.sum(full, axis=1, keepdims=True)
            at_first = jnp.sum(jnp.where(slot == 0, src, 0), axis=1, keepdims=True)
            at_pad = jnp.sum(jnp.where(slot == filled, src, 0), axis=1, keepdims=True)
            marks = (filled, at_first >> 1, at_first & 1, at_pad >> 1, at_pad & 1)
            for index, mark in enumerate(marks):
                tail = jnp.where(lane == 2 + 2 * index + buffer, mark.astype(F32), tail)
        q, k, v = q_ref[...].astype(F32), k_ref[...].astype(F32), v_ref[...].astype(F32)
        o, g, u = o_ref[...].astype(F32), g_ref[...].astype(F32), u_ref[...].astype(F32)
        sides = []
        for side in range(2):
            padded = jnp.concatenate(
                [o[:, side * half : (side + 1) * half], jnp.zeros((own, 64), F32)], axis=1
            )
            sides.append([padded[:, 128 * i : 128 * (i + 1)] for i in range(5)])
        for rank in range(RANKS):
            blocks = [
                q[:, q_cut * rank : q_cut * rank + 128],
                jnp.concatenate(
                    [
                        q[:, q_cut * rank + 128 : q_cut * (rank + 1)],
                        k[:, k_cut * rank : k_cut * (rank + 1)],
                        v[:, k_cut * rank : k_cut * (rank + 1)],
                        tail,
                    ],
                    axis=1,
                ),
            ]
            for weight in (g, u):
                cut = jnp.concatenate(
                    [
                        weight[:, low : low + piece]
                        for low in range(piece * rank, RANKS * rank_cut, RANKS * piece)
                    ],
                    axis=1,
                )
                blocks += [cut[:, 128 * i : 128 * (i + 1)] for i in range(rank_cut // 128)]
            out_ref[rank] = packed(blocks + sides[rank // DEPTHS])

    rows = own * BLOCKS
    return run(
        3.2, kernel,
        [((RANKS, rows + -rows % 8, 128), BF)],
        values,
        vmem=60,
        fetch=True,
    )[0]


def assemble(column, own, blocks, down=None):
    wide = 128 * len(blocks)
    third = 0 if down is None else down.shape[1] // 3
    rows = RANKS * own

    def kernel(column_ref, *refs):
        out_ref = refs[-1]
        parts = []
        for block in blocks:
            parts.append(
                jnp.concatenate(
                    [
                        column_ref[rank, block * own : (block + 1) * own].astype(F32)
                        for rank in range(RANKS)
                    ],
                    axis=0,
                ).astype(BF)
            )
        if down is not None:
            parts.append(
                jnp.concatenate(
                    [refs[0][:, third * i : third * (i + 1)] for i in range(3)], axis=0
                )
            )
        whole = jnp.concatenate(parts, axis=1)
        for plane in range(PLANES):
            out_ref[plane] = whole

    return run(
        1.2, kernel,
        [((PLANES, rows, wide + third), BF)],
        [column] if down is None else [column, down],
    )[0]


def unpack_down(gathered, rank_rows, wide):
    planes, rows, columns = gathered.shape
    third = columns - wide

    def kernel(in_ref, out_ref):
        for plane in range(planes):
            for part in range(3):
                out_ref[
                    plane * rank_rows : (plane + 1) * rank_rows, third * part : third * (part + 1)
                ] = in_ref[plane, part * rank_rows : (part + 1) * rank_rows, wide:]

    return run(1.9, kernel, [((planes * rank_rows, 3 * third), BF)], [gathered])[0]


def sum_ffn(received, rank_rows, wide):
    planes, rows, columns = received.shape
    third = columns - wide

    def kernel(in_ref, sum_ref, down_ref):
        total = in_ref[0].astype(F32)
        for plane in range(1, planes):
            total = total + in_ref[plane].astype(F32)
        sum_ref[...] = total[:, :wide]
        for part in range(3):
            down_ref[:, third * part : third * (part + 1)] = total[
                part * rank_rows : (part + 1) * rank_rows, wide:
            ]

    return run(0.8, kernel, [((rows, wide), F32), ((rank_rows, 3 * third), F32)], [received])


def send_sums(attention, ffn, own):
    def kernel(attention_ref, ffn_ref, out_ref):
        total = attention_ref[0].astype(F32)
        for plane in range(1, PLANES):
            total = total + attention_ref[plane].astype(F32)
        wholes = [total[:, :256], ffn_ref[...], total[:, 256:]]
        for rank in range(RANKS):
            at = slice(rank * own, (rank + 1) * own)
            out_ref[rank] = packed(
                [
                    whole[at, 128 * i : 128 * (i + 1)]
                    for whole in wholes
                    for i in range(whole.shape[1] // 128)
                ]
            )

    rows = own * BLOCKS
    return run(
        2.7, kernel, [((RANKS, rows + -rows % 8, 128), BF)], [attention, ffn]
    )[0]


def finish(received, first_gain, second_gain, query, key, value, gate, up):
    own, width = query.shape
    q_cut, k_cut = width // RANKS, key.shape[1] // RANKS
    rank_cut = gate.shape[1] // RANKS
    piece = rank_cut // PLANES
    half = width // 2

    def kernel(in_ref, one_ref, two_ref, q_in, k_in, v_in, g_in, u_in, *outs):
        one_out, q_out, k_out, v_out, o_out, two_out, g_out, u_out = outs

        def block(rank, index):
            return in_ref[rank, index * own : (index + 1) * own].astype(F32)

        second = [block(rank, 1) for rank in range(RANKS)]
        q_parts = []
        for rank in range(RANKS):
            q_parts += [block(rank, 0), second[rank][:, : q_cut - 128]]
        low = q_cut - 128
        q = jnp.concatenate(q_parts, axis=1)
        k = jnp.concatenate([part[:, low : low + k_cut] for part in second], axis=1)
        v = jnp.concatenate([part[:, low + k_cut : low + 2 * k_cut] for part in second], axis=1)
        q_out[...], k_out[...], v_out[...] = q, k, v
        ffn = []
        for base in (2, 2 + rank_cut // 128):
            wide = [
                jnp.concatenate([block(rank, base + i) for i in range(rank_cut // 128)], axis=1)
                for rank in range(RANKS)
            ]
            ffn.append(
                jnp.concatenate(
                    [
                        wide[rank][:, piece * plane : piece * (plane + 1)]
                        for plane in range(PLANES)
                        for rank in range(RANKS)
                    ],
                    axis=1,
                )
            )
        g_out[...], u_out[...] = ffn
        base = 2 + 2 * rank_cut // 128
        sides = []
        for side in range(2):
            parts = []
            for i in range(base, BLOCKS):
                total = block(side * DEPTHS, i)
                for step in range(1, DEPTHS):
                    total = total + block(side * DEPTHS + step, i)
                parts.append(total)
            sides.append(jnp.concatenate(parts, axis=1)[:, :half])
        o_out[...] = jnp.concatenate(sides, axis=1)

        def along(pairs):
            return sum(
                jnp.sum(grad * ref[...].astype(F32), axis=1, keepdims=True) for grad, ref in pairs
            )

        def as_row(column):
            rows = lax.broadcasted_iota(jnp.int32, (own, own), 0)
            columns = lax.broadcasted_iota(jnp.int32, (own, own), 1)
            return jnp.sum(jnp.where(rows == columns, column, 0.0), axis=0, keepdims=True)

        one_out[...] = as_row(along([(q, q_in), (k, k_in), (v, v_in)])) / one_ref[...].astype(F32)
        two_out[...] = as_row(along([(ffn[0], g_in), (ffn[1], u_in)])) / two_ref[...].astype(F32)

    return run(
        1.3, kernel,
        [
            ((1, own), F32),
            (query.shape, F32),
            (key.shape, F32),
            (value.shape, F32),
            (query.shape, F32),
            ((1, own), F32),
            (gate.shape, F32),
            (up.shape, F32),
        ],
        [received, first_gain, second_gain, query, key, value, gate, up],
    )


def norm_back(grad, normed, scale):
    return scale * (grad - normed * jnp.mean(grad * normed, axis=-1, keepdims=True))


def on_device(
    tokens,
    cotangent,
    segments,
    slot_source,
    first_gain,
    query_weight,
    key_projection,
    value_projection,
    output_weight,
    second_gain,
    gate_weight,
    up_weight,
    down_weight,
):
    core, depth = lax.axis_index("c"), lax.axis_index("z")
    rows, width = tokens.shape
    own = query_weight.shape[0]
    q_cut, k_cut = query_weight.shape[1] // RANKS, key_projection.shape[1] // RANKS
    rank_rows = down_weight.shape[0]
    wide = 2 * gate_weight.shape[1] // RANKS
    cut = q_cut + 2 * k_cut
    gain_one, gain_two = first_gain.reshape(1, own), second_gain.reshape(1, own)

    def column_blocks(value):
        mine = gather_depths(value)
        return mine, [exchange(block) for block in mine]

    def parcels_between(parcels):
        mine = scatter_depths(parcels)
        return mine, [exchange(block) for block in mine]

    inputs_mine, inputs_theirs = column_blocks(tokens)
    column = deal(
        prepare(
            segments[0],
            slot_source[0],
            gain_one,
            gain_two,
            query_weight,
            key_projection,
            value_projection,
            output_weight,
            gate_weight,
            up_weight,
        ),
        COLUMN,
    )
    attention_w = deal(assemble(column, own, range(2)), PLANE).reshape(width, -1)
    output_in = assemble(column, own, range(8, BLOCKS))
    ffn_in = assemble(column, own, range(2, 8), down_weight)

    marks = column.reshape(2, DEPTHS, -1, 128)[:, :, own, cut + 2 - 128 : cut + 12 - 128]
    marks = marks.astype(jnp.int32)
    marks = jnp.where(core == 0, marks[0], marks[1]).reshape(DEPTHS, 5, 2)
    padded = marks[:, 0] < segments.shape[2]
    earlier_padded = jnp.concatenate([jnp.zeros((1, 2), bool), padded[:-1]])
    pad_starts = jnp.sum(
        jnp.where(padded & ~earlier_padded, marks[:, 3] * 2 + marks[:, 4], 0), axis=0
    )
    starts = jnp.concatenate([marks[0, 1] * 2 + marks[0, 2], pad_starts])
    group_rows = jnp.arange(DEPTHS * rows)
    run_start = jnp.max(
        jnp.where(starts[None, :] <= group_rows[:, None], starts[None, :], 0), axis=1
    )
    frequency = THETA ** (-(jnp.arange(HEAD // 2).astype(F32) * 2.0 / HEAD))
    angles = frequency[:, None] * (group_rows - run_start).astype(F32)[None, :]
    cosine, sine = jnp.cos(angles), jnp.sin(angles)
    place = jnp.concatenate([jnp.stack([core, depth]), starts]).astype(jnp.int32)

    hidden_one, gains_full, *parcels = project(
        after(place, (cosine, sine)), inputs_mine + inputs_theirs, attention_w, cut, q_cut
    )
    output_own = deal(after(output_in, parcels[0]), PLANE)
    mine, theirs = parcels_between(parcels)
    upstream_mine = gather_depths(after(cotangent, theirs[3]))
    ffn_blocks = deal(after(ffn_in, (output_own, theirs)), PLANE)
    output_own = output_own.reshape(width, -1)
    output_other = exchange(output_own)
    down_w = unpack_down(ffn_blocks, rank_rows, wide)
    ffn_w = ffn_blocks.reshape(width, -1)
    query, key, value, stats, mixed = attend(place, mine, theirs, cosine, sine, q_cut, k_cut)

    residual, hidden_two = into_residual(
        place, mixed, tokens, output_own, output_other, gains_full
    )
    mixed_other = exchange(mixed)
    hidden_mine, hidden_theirs = column_blocks(after(hidden_two, mixed_other))
    upstream_theirs = [exchange(after(block, hidden_mine)) for block in upstream_mine]
    inner_theirs, grads_theirs, partial_theirs = feed_forward(
        hidden_theirs, upstream_theirs, ffn_w, down_w, BF
    )
    inner_mine, grads_mine, partial_mine = feed_forward(
        hidden_mine, upstream_mine, ffn_w, down_w, F32
    )
    ffn_grads = ffn_gradients(
        hidden_mine + hidden_theirs,
        [grads_mine, grads_theirs],
        [inner_mine, inner_theirs],
        upstream_mine + upstream_theirs,
    )
    parts = scatter_depths(add_sides(partial_mine, exchange(partial_theirs)))
    grad_residual, residual_low, grad_mixed = residual_back(
        after(place, ffn_grads), parts, residual, cotangent, output_own, output_other, gains_full
    )
    ffn_sum = deal(ffn_grads, PLANE)

    parcels = attend_back(
        place, query, key, value, stats, grad_mixed, cosine, sine, q_cut, k_cut
    )
    mine, theirs = parcels_between(parcels)
    output_grads = output_gradient(
        place,
        mixed,
        mixed_other,
        after(residual_low, parcels[0]),
        exchange(residual_low),
        output_own.shape[1],
    )
    projected_rows, attention_grads = project_back(
        place, mine, theirs, hidden_one, output_grads, q_cut, k_cut
    )
    attention_sum = deal(after(attention_grads, ffn_sum), PLANE)
    outputs_own, outputs_other = side_outputs(
        after(inner_mine, attention_grads), inner_theirs, down_w
    )
    outputs = add_sides(outputs_own, exchange(outputs_other))
    inputs_own, inputs_other = side_product(projected_rows, attention_w)
    parts = scatter_depths(add_sides(inputs_own, exchange(inputs_other)))
    gradient_tokens = inputs_back(parts, tokens, grad_residual, gains_full)
    outputs = [outputs[0]] + [after(part, parts[1:3]) for part in outputs[1:]]
    outputs = scatter_depths(outputs)
    layer_output = (residual + sum(part.astype(F32) for part in outputs)).astype(BF)

    ffn_sum, grad_down = sum_ffn(ffn_sum, rank_rows, wide)
    received = deal(send_sums(attention_sum, ffn_sum, own), COLUMN)
    one, grad_q, grad_k, grad_v, grad_o, two, grad_g, grad_u = finish(
        received,
        gain_one,
        gain_two,
        query_weight,
        key_projection,
        value_projection,
        gate_weight,
        up_weight,
    )
    return (
        layer_output,
        gradient_tokens,
        one.reshape(own),
        grad_q,
        grad_k,
        grad_v,
        grad_o,
        two.reshape(own),
        grad_g,
        grad_u,
        grad_down,
    )


def solution(mesh):
    grid = Mesh(mesh.devices.reshape(4, 4, 2, 4), ALL)
    rows = P(ALL, None)
    flat = P(ALL)
    slots = P(("y", "x", "c"), None, "z")
    return jax.shard_map(
        on_device,
        mesh=grid,
        in_specs=(rows, rows, slots, slots, flat, rows, rows, rows, rows, flat, rows, rows, rows),
        out_specs=(rows, rows, flat, rows, rows, rows, rows, flat, rows, rows, rows),
        check_vma=False,
    )
```
